32 devices in a mesh: row: 4 (over y, x), col: 8 (over z, core).
Axes of the slice: x: 2, y: 2, z: 4, core: 2. Of those that a mesh axis runs over, the one named last changes fastest.
Arguments:
- layer_input: bfloat16 [640, 8192], P('col', 'row'), may hold values from -6 to 6
- w_query: bfloat16 [8192, 8192], P('row', 'col'), may hold values from -0.0625 to 0.0625
- w_key: bfloat16 [8192, 1024], P('row', 'col'), may hold values from -0.0625 to 0.0625
- w_value: bfloat16 [8192, 1024], P('row', 'col'), may hold values from -0.0625 to 0.0625
- rotated_query_state: bfloat16 [640, 8192], P('row', 'col'), may hold values from -156 to 156
- rotated_key_state: bfloat16 [640, 1024], P('row', 'col'), may hold values from -6 to 6
- saved_value_state: bfloat16 [640, 1024], P('row', 'col'), may hold values from -6 to 6
- context_gradient: bfloat16 [640, 8192], P('row', 'col'), may hold values from -24 to 24
- positions: int32 [640], P('row'), may hold values from 0 to 542, as said below
- segment_ids: int32 [640], P('row'), may hold values from 0 to 1, as said below
Outputs:
- grad_input: bfloat16 [640, 8192], P('col', 'row')
- grad_wq: float32 [8192, 8192], P('row', 'col')
- grad_wk: float32 [8192, 1024], P('row', 'col')
- grad_wv: float32 [8192, 1024], P('row', 'col')
The draws below stay inside these ranges and needn't reach their ends.
Inputs may be any that keep to these rules, and one draw needn't show every extreme that they name: `segment_ids`: never falls along the tokens; each of the 2 rollouts holds at least one token. `positions`: rises by one from each token to the next within a rollout.
All inputs are finite; a program needn't handle non-finite values.
Results may differ from the reference program's by a relative error of at most 0.025.
Values may be sent and summed in bfloat16 or wider, within the bound.
No kernel may reach another device: no remote copies, remote signals or barrier semaphores. Data moves between devices by JAX's collectives and lax.ppermute only.
A program may use at most 128 MiB of HBM per device.

```python
import math
import jax
import jax.numpy as jnp
from jax import lax

D = 8192
QUERY_HEADS = 64
KEY_VALUE_HEADS = 8
HEAD_SIZE = 128
TOK_DEV = 160
ROLLOUTS = 2
BATCH_TOKENS = 640
QUERY_FEATURES = 8192
KD = 1024
N_ROW = 4
N_COL = 8


def rollout_layout(key):
    jitter_reach = BATCH_TOKENS // (4 * ROLLOUTS)
    jitter = jax.random.randint(jax.random.fold_in(key, 11), (ROLLOUTS - 1,), -jitter_reach, jitter_reach + 1)
    cut_points = (jnp.arange(1, ROLLOUTS, dtype=jnp.int32) * (BATCH_TOKENS // ROLLOUTS) + jitter).astype(jnp.int32)
    token_index = jnp.arange(BATCH_TOKENS, dtype=jnp.int32)
    rollout_ids = jnp.sum((token_index[:, None] >= cut_points[None, :]).astype(jnp.int32), axis=1)
    starts = jnp.concatenate([jnp.zeros((1,), jnp.int32), cut_points])
    random_shift = jax.random.randint(jax.random.fold_in(key, 12), (ROLLOUTS,), 0, 64).astype(jnp.int32)
    top_position = BATCH_TOKENS // ROLLOUTS + 2 * jitter_reach + 62
    first_shift = (top_position + 1 - cut_points[0]).astype(jnp.int32)
    rollout_index = jnp.arange(ROLLOUTS, dtype=jnp.int32)
    prompt_shift = jnp.where(rollout_index == 0, first_shift, jnp.where(rollout_index == ROLLOUTS - 1, 0, random_shift)).astype(jnp.int32)
    onehot = (rollout_ids[:, None] == rollout_index[None, :]).astype(jnp.int32)
    begin_index = jnp.sum(onehot * starts[None, :], axis=1)
    shift_here = jnp.sum(onehot * prompt_shift[None, :], axis=1)
    return (rollout_ids.astype(jnp.int32), (token_index - begin_index + shift_here).astype(jnp.int32))


def drawn_pair(key, strength):
    base_query = jnp.clip(jax.random.normal(jax.random.fold_in(key, 21), (BATCH_TOKENS, QUERY_FEATURES), jnp.float32), -6.0, 6.0)
    base_key = jnp.clip(jax.random.normal(jax.random.fold_in(key, 22), (BATCH_TOKENS, KD), jnp.float32), -6.0, 6.0)
    token_index = jnp.arange(BATCH_TOKENS)
    anchor = (token_index % 61 == 30).astype(jnp.float32) * strength
    before = jnp.roll(anchor, -1)
    follow = jnp.roll(base_key, -1, axis=0)
    key_token_rows = base_key * (1.0 - before[:, None]) + 0.99 * follow * before[:, None]
    query_rows = base_query * (1.0 - anchor[:, None])
    return (query_rows, key_token_rows)


def draw_segment_ids(key, part):
    rollout_ids, position_rows = rollout_layout(key)
    return rollout_ids


def draw_positions(key, part):
    rollout_ids, position_rows = rollout_layout(key)
    return position_rows


def draw_rotated_query_state(key, part):
    query_rows, key_token_rows = drawn_pair(key, 0.0)
    return query_rows.astype(jnp.bfloat16)


def draw_rotated_key_state(key, part):
    query_rows, key_token_rows = drawn_pair(key, 0.0)
    return key_token_rows.astype(jnp.bfloat16)


def steps_of(key, dims, cuts, low, largest):
    loudness, own = 1.0, jax.random.fold_in(key, 6)
    for axis_at, blocks in cuts:
        steps = jnp.exp(jax.random.uniform(jax.random.fold_in(own, axis_at), (blocks,), jnp.float32, low / len(cuts), largest / len(cuts)))
        loudness = loudness * jnp.repeat(steps, dims[axis_at] // blocks).reshape([-1 if axis == axis_at else 1 for axis in range(len(dims))])
    return loudness


def noise(key, shape, deviation, bound, split=(), kind=jnp.bfloat16):
    drawn = deviation * jax.random.normal(key, shape, jnp.float32)
    if split:
        drawn = drawn * steps_of(key, shape, split, -0.22, 0.18)
    return jnp.clip(drawn, -bound, bound).astype(kind)


def setup_inputs(seed: int = 0) -> dict:
    splits = jax.random.split(jax.random.key(seed), 11)
    layer_input = noise(splits[0], (BATCH_TOKENS, D), 1.0, 6.0, ((0, 8), (1, 4)))
    w_query = noise(splits[1], (D, QUERY_FEATURES), D ** -0.5, 0.0625, ((0, 4), (1, 8)))
    w_key = noise(splits[2], (D, KD), D ** -0.5, 0.0625, ((0, 4), (1, 8)))
    w_value = noise(splits[3], (D, KD), D ** -0.5, 0.0625, ((0, 4), (1, 8)))
    rotated_query_state = draw_rotated_query_state(jax.random.fold_in(splits[10], 71), 0)
    rotated_key_state = draw_rotated_key_state(jax.random.fold_in(splits[10], 71), 0)
    saved_value_state = noise(splits[6], (BATCH_TOKENS, KD), 1.0, 6.0, ((0, 4), (1, 8)))
    context_gradient = noise(splits[7], (BATCH_TOKENS, QUERY_FEATURES), 4.0, 24.0, ((0, 4), (1, 8)))
    positions = draw_positions(jax.random.fold_in(splits[10], 71), 0)
    segment_ids = draw_segment_ids(jax.random.fold_in(splits[10], 71), 0)
    return dict(layer_input=layer_input, w_query=w_query, w_key=w_key, w_value=w_value, rotated_query_state=rotated_query_state, rotated_key_state=rotated_key_state, saved_value_state=saved_value_state, context_gradient=context_gradient, positions=positions, segment_ids=segment_ids)


rope_base = 500000.0


def contract(left, right, left_dim, right_dim):
    return lax.dot_general(left, right, (((left_dim,), (right_dim,)), ((), ())), preferred_element_type=jnp.float32)


def rope_tables(positions):
    half_width = HEAD_SIZE // 2
    freq = jnp.exp(-(2.0 * jnp.arange(half_width, dtype=jnp.float32) / HEAD_SIZE) * math.log(rope_base))
    angle = positions.astype(jnp.float32)[:, None] * freq[None, :]
    return jnp.cos(angle), jnp.sin(angle)


def unrotate(gradient, cosine, sine):
    half_width = gradient.shape[-1] // 2
    first = gradient[..., :half_width]
    second = gradient[..., half_width:]
    return jnp.concatenate([first * cosine + second * sine, second * cosine - first * sine], axis=-1)


def blocked_partials(left, right, shared_heads, per_share):
    left_blocks = left.astype(jnp.float32).reshape(shared_heads, per_share, N_ROW, TOK_DEV, BATCH_TOKENS)
    right_blocks = right.astype(jnp.float32).reshape(shared_heads, per_share, N_ROW, TOK_DEV, HEAD_SIZE)
    parts = jnp.einsum("jhbts,jhbtd->jbsd", left_blocks, right_blocks)
    rounded = lax.optimization_barrier(parts.astype(jnp.bfloat16)).astype(jnp.float32)
    return jnp.sum(rounded, axis=(0, 1))


def reference(layer_input, w_query, w_key, w_value, rotated_query_state, rotated_key_state, saved_value_state, context_gradient, positions, segment_ids):
    score_scale = HEAD_SIZE ** -0.5
    heads_per_group = QUERY_HEADS // KEY_VALUE_HEADS
    shared_heads = N_COL // KEY_VALUE_HEADS
    per_share = heads_per_group // shared_heads
    visible = (segment_ids[:, None] == segment_ids[None, :]) & (positions[None, :] <= positions[:, None])
    query_grouped = rotated_query_state.reshape(BATCH_TOKENS, KEY_VALUE_HEADS, heads_per_group * HEAD_SIZE).transpose(1, 0, 2)
    gradient_grouped = context_gradient.reshape(BATCH_TOKENS, KEY_VALUE_HEADS, heads_per_group * HEAD_SIZE).transpose(1, 0, 2)
    key_grouped = rotated_key_state.reshape(BATCH_TOKENS, KEY_VALUE_HEADS, HEAD_SIZE).transpose(1, 0, 2)
    value_grouped = saved_value_state.reshape(BATCH_TOKENS, KEY_VALUE_HEADS, HEAD_SIZE).transpose(1, 0, 2)

    def one_group(operands):
        query_part, grad_part, key_part, value_part = operands
        query_rows = query_part.reshape(BATCH_TOKENS, heads_per_group, HEAD_SIZE).transpose(1, 0, 2).reshape(heads_per_group * BATCH_TOKENS, HEAD_SIZE)
        grad_rows = grad_part.reshape(BATCH_TOKENS, heads_per_group, HEAD_SIZE).transpose(1, 0, 2).reshape(heads_per_group * BATCH_TOKENS, HEAD_SIZE)
        scores = (contract(query_rows, key_part, 1, 1) * score_scale).reshape(heads_per_group, BATCH_TOKENS, BATCH_TOKENS)
        row_peak = jnp.max(jnp.where(visible[None], scores, -1e30), axis=-1, keepdims=True)
        exponent_terms = jnp.where(visible[None], jnp.exp(scores - row_peak), 0.0)
        weights = exponent_terms / jnp.sum(exponent_terms, axis=-1, keepdims=True)
        weights_low = weights.astype(jnp.bfloat16)
        dweights = contract(grad_rows, value_part, 1, 1).reshape(heads_per_group, BATCH_TOKENS, BATCH_TOKENS)
        row_delta = jnp.sum(weights * dweights, axis=-1, keepdims=True)
        dscores = (weights * (dweights - row_delta) * score_scale).astype(jnp.bfloat16)
        flat_dscores = dscores.reshape(heads_per_group * BATCH_TOKENS, BATCH_TOKENS)
        dquery_rot = contract(flat_dscores, key_part, 1, 0).reshape(heads_per_group, BATCH_TOKENS, HEAD_SIZE).transpose(1, 0, 2)
        dkey_rot = blocked_partials(dscores, query_rows, shared_heads, per_share)
        dvalue = blocked_partials(weights_low, grad_rows, shared_heads, per_share)
        return dquery_rot, dkey_rot, dvalue

    dquery_rot, dkey_rot, dvalue = lax.map(one_group, (query_grouped, gradient_grouped, key_grouped, value_grouped))
    dquery_rot = dquery_rot.transpose(1, 0, 2, 3).reshape(BATCH_TOKENS, QUERY_HEADS, HEAD_SIZE)
    dkey_rot = dkey_rot.transpose(1, 0, 2)
    cosine, sine = rope_tables(positions)
    dquery = unrotate(dquery_rot, cosine[:, None], sine[:, None]).reshape(BATCH_TOKENS, QUERY_FEATURES).astype(jnp.bfloat16)
    dkey = unrotate(dkey_rot, cosine[:, None], sine[:, None]).reshape(BATCH_TOKENS, KD).astype(jnp.bfloat16)
    dvalue_low = dvalue.transpose(1, 0, 2).reshape(BATCH_TOKENS, KD).astype(jnp.bfloat16)
    grad_wq = contract(layer_input, dquery, 0, 0)
    grad_wk = contract(layer_input, dkey, 0, 0)
    grad_wv = contract(layer_input, dvalue_low, 0, 0)
    query_cols = QUERY_FEATURES // N_COL
    key_cols = KD // N_COL
    grad_blocks = jnp.concatenate([dquery.reshape(BATCH_TOKENS, N_COL, query_cols), dkey.reshape(BATCH_TOKENS, N_COL, key_cols), dvalue_low.reshape(BATCH_TOKENS, N_COL, key_cols)], axis=2).transpose(1, 0, 2)
    weight_blocks = jnp.concatenate([w_query.reshape(D, N_COL, query_cols), w_key.reshape(D, N_COL, key_cols), w_value.reshape(D, N_COL, key_cols)], axis=2).transpose(1, 0, 2)

    def accumulate(running, operands):
        grad_block, weight_block = operands
        partial_sum = contract(grad_block, weight_block, 1, 1)
        rounded = lax.optimization_barrier(partial_sum.astype(jnp.bfloat16)).astype(jnp.float32)
        return running + rounded, None

    summed, unused_out = lax.scan(accumulate, jnp.zeros((BATCH_TOKENS, D), jnp.float32), (grad_blocks, weight_blocks))
    return summed.astype(jnp.bfloat16), grad_wq, grad_wk, grad_wv
```

```python
import functools
import math

import jax
import jax.numpy as jnp
import numpy as np
from jax import lax
from jax.experimental import pallas as pl
from jax.experimental.pallas import tpu as pltpu
from jax.sharding import PartitionSpec as P

KEY_VALUE_HEADS = 8
HEAD_SIZE = 128
ROPE_BASE = 500000.0
PAD_ROWS = 16
MIB = 1024 * 1024


def contract(left, right, left_dim, right_dim):
    return lax.dot_general(
        left, right, (((left_dim,), (right_dim,)), ((), ())), preferred_element_type=jnp.float32
    )


def swap(value, axis, offset):
    pairs = [(source, source ^ offset) for source in range(lax.axis_size(axis))]
    return lax.ppermute(value, axis, pairs)


def gather_direct(value, axis):
    return [value] + [swap(value, axis, s) for s in range(1, lax.axis_size(axis))]


def add_low(left, right):
    return (left.astype(jnp.float32) + right.astype(jnp.float32)).astype(jnp.bfloat16)


def block_index(position, row, blocks, tokens):
    index = position
    for b in range(blocks):
        index = jnp.where(position >= b * tokens, position + ((row ^ b) - b) * tokens, index)
    return index.astype(jnp.float32)


def unrotate(gradient, cosine, sine):
    return gradient * cosine + pltpu.roll(gradient, HEAD_SIZE // 2, 1) * sine


def pack_kernel(k_ref, v_ref, ids_ref, out_ref):
    tokens = k_ref.shape[0]
    out_ref[:tokens, :HEAD_SIZE] = k_ref[...]
    out_ref[:tokens, HEAD_SIZE:] = v_ref[...]
    width = ids_ref.shape[1]
    row = lax.broadcasted_iota(jnp.int32, (PAD_ROWS, width), 0)
    ids = jnp.ones((PAD_ROWS, width), jnp.float32)
    for i in range(ids_ref.shape[0]):
        ids = jnp.where(row == i, ids_ref[i : i + 1, :].astype(jnp.float32), ids)
    out_ref[tokens:, :] = jnp.ones((PAD_ROWS, out_ref.shape[1]), jnp.bfloat16)
    out_ref[tokens:, :width] = ids.astype(jnp.bfloat16)


def pack(key, value, segment_ids):
    tokens = key.shape[0]
    width = 2 * HEAD_SIZE
    rows = -(-tokens // width)
    ids = segment_ids
    if rows > 1:
        ids = jnp.pad(ids, (0, rows * width - tokens), constant_values=1)
    ids = ids.reshape(rows, -1)
    vmem = pl.BlockSpec(memory_space=pltpu.VMEM)
    return pl.pallas_call(
        pack_kernel,
        out_shape=jax.ShapeDtypeStruct((tokens + PAD_ROWS, width), jnp.bfloat16),
        in_specs=[vmem] * 3,
        out_specs=vmem,
        compiler_params=pltpu.CompilerParams(vmem_limit_bytes=MIB),
        cost_estimate=pl.CostEstimate(
            flops=0, bytes_accessed=8 * tokens * HEAD_SIZE, transcendentals=0
        ),
        name="pack",
    )(
        pltpu.with_memory_space_constraint(key, pltpu.HBM),
        pltpu.with_memory_space_constraint(value, pltpu.HBM),
        pltpu.with_memory_space_constraint(ids, pltpu.HBM),
    )


def prepare_kernel(heads, blocks, row_ref, q_hbm, o_hbm, positions_ref, ids_ref, freq_ref, *refs):
    q_ref, o_ref, cos_ref, sin_ref, sems = refs
    tokens = q_hbm.shape[0]
    row = row_ref[0]
    copies = []
    for h in range(heads):
        rows = slice(h * tokens, (h + 1) * tokens)
        cols = slice(h * HEAD_SIZE, (h + 1) * HEAD_SIZE)
        for i, (source, target) in enumerate(((q_hbm, q_ref), (o_hbm, o_ref))):
            copies.append(
                pltpu.make_async_copy(source.at[:, cols], target.at[rows, :], sems.at[h, i])
            )
            copies[-1].start()

    first = (row * tokens).astype(jnp.float32)
    last = first + (tokens - 1)
    positions = positions_ref[...].astype(jnp.float32)
    cut = first + jnp.sum(1.0 - ids_ref[...].astype(jnp.float32), axis=1, keepdims=True)
    offset_low = positions[:, :1] - first
    offset_high = positions[:, tokens - 1 :] - last
    place = lax.broadcasted_iota(jnp.int32, (blocks * tokens, 1), 0)
    index = block_index(place, row, blocks, tokens)
    angle = (index + jnp.where(index < cut, offset_low, offset_high)) * freq_ref[...]
    lane = lax.broadcasted_iota(jnp.int32, (1, HEAD_SIZE), 1)
    lower = lane < HEAD_SIZE // 2
    table = jnp.cos(angle - jnp.where(lower, 0.0, math.pi / 2))
    turned = pltpu.roll(table, HEAD_SIZE // 2, 1)
    cos_ref[...] = jnp.where(lower, table, turned)
    sin_ref[...] = jnp.where(lower, turned, -table)

    for copy in copies:
        copy.wait()


def prepare(row, blocks, query, out_grad, positions, segment_ids):
    tokens, width = query.shape
    heads = width // HEAD_SIZE
    half_width = HEAD_SIZE // 2
    freq = np.exp(-(2.0 * np.arange(half_width) / HEAD_SIZE) * math.log(ROPE_BASE))
    freq = np.tile(freq, 2)[None].astype(np.float32)
    vmem = pl.BlockSpec(memory_space=pltpu.VMEM)
    hbm = pl.BlockSpec(memory_space=pltpu.HBM)
    return pl.pallas_call(
        functools.partial(prepare_kernel, heads, blocks),
        out_shape=[jax.ShapeDtypeStruct((heads * tokens, HEAD_SIZE), jnp.bfloat16)] * 2
        + [jax.ShapeDtypeStruct((blocks * tokens, HEAD_SIZE), jnp.float32)] * 2,
        in_specs=[pl.BlockSpec(memory_space=pltpu.SMEM), hbm, hbm, vmem, vmem, vmem],
        out_specs=[vmem] * 4,
        scratch_shapes=[pltpu.SemaphoreType.DMA((heads, 2))],
        compiler_params=pltpu.CompilerParams(vmem_limit_bytes=8 * MIB),
        cost_estimate=pl.CostEstimate(
            flops=0,
            bytes_accessed=8 * tokens * width,
            transcendentals=2 * blocks * tokens * HEAD_SIZE,
        ),
        name="prepare",
    )(
        row,
        pltpu.with_memory_space_constraint(query, pltpu.HBM),
        pltpu.with_memory_space_constraint(out_grad, pltpu.HBM),
        pltpu.with_memory_space_constraint(positions.reshape(1, -1), pltpu.HBM),
        pltpu.with_memory_space_constraint(segment_ids.reshape(1, -1), pltpu.HBM),
        pltpu.with_memory_space_constraint(jnp.asarray(freq), pltpu.HBM),
    )


def attention_kernel(heads, blocks, row_ref, q_all, o_all, *refs):
    kv_refs = refs[:blocks]
    cos_ref, sin_ref = refs[blocks : blocks + 2]
    dq_refs, packet_refs = refs[blocks + 2 : blocks + 4], refs[blocks + 4 : blocks + 6]
    k_all, v_all, ds_all, w_all, bias_ref, scores_ref, dweights_ref = refs[blocks + 6 :]
    together = scores_ref.shape[0] // bias_ref.shape[0]
    tokens = q_all.shape[0] // heads
    width = dq_refs[0].shape[1]
    keys = tokens * blocks
    scale = HEAD_SIZE**-0.5
    row = row_ref[0]

    cut = jnp.zeros((1, 1), jnp.float32)
    for b in range(blocks):
        rows = slice(b * tokens, (b + 1) * tokens)
        k_all[rows, :] = kv_refs[b][:tokens, :HEAD_SIZE]
        v_all[rows, :] = kv_refs[b][:tokens, HEAD_SIZE:]
        first = 1.0 - kv_refs[b][tokens:, :].astype(jnp.float32)
        cut += jnp.sum(jnp.sum(first, axis=0, keepdims=True), axis=1, keepdims=True)
    lane = lax.broadcasted_iota(jnp.int32, (1, keys), 1)
    key_index = block_index(lane, row, blocks, tokens)
    query_index = (
        lax.broadcasted_iota(jnp.int32, (tokens, 1), 0) + row * tokens
    ).astype(jnp.float32)
    lowest = jnp.where(query_index < cut, 0.0, cut)
    visible = (key_index <= query_index) & (key_index >= lowest)
    bias_ref[...] = jnp.where(visible, 0.0, -1e30)

    for h in range(heads):
        if h % together == 0:
            rows = slice(h * tokens, (h + together) * tokens)
            scores_ref[...] = contract(q_all[rows, :], k_all[...], 1, 1)
            dweights_ref[...] = contract(o_all[rows, :], v_all[...], 1, 1)
        rows = slice(h % together * tokens, (h % together + 1) * tokens)
        scores = scores_ref[rows, :] + bias_ref[...]
        peak = jnp.max(scores, axis=1, keepdims=True)
        terms = jnp.exp2((scores - peak) * (scale * math.log2(math.e)))
        inverse = 1.0 / jnp.sum(terms, axis=1, keepdims=True)
        dweights = dweights_ref[rows, :]
        weights = terms * inverse
        delta = jnp.sum(weights * dweights, axis=1, keepdims=True)
        dscores = (weights * (dweights - delta) * scale).astype(jnp.bfloat16)
        rows = slice(h * tokens, (h + 1) * tokens)
        w_all[rows, :] = weights.astype(jnp.bfloat16)
        ds_all[rows, :] = dscores
    dq = contract(ds_all[...], k_all[...], 1, 0)
    for h in range(heads):
        side, first = divmod(h * HEAD_SIZE, width)
        cols = slice(first, first + HEAD_SIZE)
        head = dq[h * tokens : (h + 1) * tokens]
        head = unrotate(head, cos_ref[:tokens, :], sin_ref[:tokens, :]).astype(jnp.bfloat16)
        dq_refs[side][:, cols] = head
        packet_refs[side][:, cols] = head
    dk = contract(ds_all[...], q_all[...], 0, 0)
    dk = unrotate(dk, cos_ref[...], sin_ref[...]).astype(jnp.bfloat16)
    dv = contract(w_all[...], o_all[...], 0, 0).astype(jnp.bfloat16)
    for b in range(blocks):
        rows = slice(b * tokens, (b + 1) * tokens)
        cols = slice(width + b * HEAD_SIZE, width + (b + 1) * HEAD_SIZE)
        packet_refs[0][:, cols] = dk[rows]
        packet_refs[1][:, cols] = dv[rows]


def attention_backward(row, query, out_grad, packed, cosine, sine):
    blocks = len(packed)
    keys = cosine.shape[0]
    tokens = keys // blocks
    heads = query.shape[0] // tokens
    width = heads // 2 * HEAD_SIZE
    vmem = pl.BlockSpec(memory_space=pltpu.VMEM)
    return pl.pallas_call(
        functools.partial(attention_kernel, heads, blocks),
        out_shape=[jax.ShapeDtypeStruct((tokens, width), jnp.bfloat16)] * 2
        + [jax.ShapeDtypeStruct((tokens, width + blocks * HEAD_SIZE), jnp.bfloat16)] * 2,
        in_specs=[pl.BlockSpec(memory_space=pltpu.SMEM)] + [vmem] * (blocks + 4),
        out_specs=[vmem] * 4,
        scratch_shapes=[
            pltpu.VMEM((keys, HEAD_SIZE), jnp.bfloat16),
            pltpu.VMEM((keys, HEAD_SIZE), jnp.bfloat16),
            pltpu.VMEM((heads * tokens, keys), jnp.bfloat16),
            pltpu.VMEM((heads * tokens, keys), jnp.bfloat16),
            pltpu.VMEM((tokens, keys), jnp.float32),
            pltpu.VMEM((min(4, heads) * tokens, keys), jnp.float32),
            pltpu.VMEM((min(4, heads) * tokens, keys), jnp.float32),
        ],
        compiler_params=pltpu.CompilerParams(vmem_limit_bytes=32 * MIB),
        cost_estimate=pl.CostEstimate(
            flops=10 * heads * tokens * keys * HEAD_SIZE,
            bytes_accessed=16 * tokens * width + 16 * keys * HEAD_SIZE,
            transcendentals=heads * tokens * keys,
        ),
        name="attention_backward",
    )(row, query, out_grad, *packed, cosine, sine)


def combine_kernel(blocks, offset, columns, width, *refs):
    packet_ref, other_ref, out_ref = refs[0], refs[1], refs[-1]
    for i, first in enumerate(columns):
        out_ref[:, i * width : (i + 1) * width] = refs[2 + i][:, first : first + width]
    for b in range(blocks):
        first = len(columns) * width + b * HEAD_SIZE
        out_ref[:, first : first + HEAD_SIZE] = summed_block(
            packet_ref, other_ref, blocks, b, offset, slice(None)
        )


def summed_block(packet_ref, other_ref, blocks, b, offset, rows):
    first = packet_ref.shape[1] - (blocks - b) * HEAD_SIZE
    total = packet_ref[rows, first : first + HEAD_SIZE].astype(jnp.float32)
    first = other_ref.shape[1] - (blocks - (b ^ offset)) * HEAD_SIZE
    total += other_ref[rows, first : first + HEAD_SIZE].astype(jnp.float32)
    return total.astype(jnp.bfloat16)


def combine(packet, other, pieces, blocks, offset, width):
    tokens = packet.shape[0]
    cols = len(pieces) * width + blocks * HEAD_SIZE
    vmem = pl.BlockSpec(memory_space=pltpu.VMEM)
    return pl.pallas_call(
        functools.partial(combine_kernel, blocks, offset, [c for _, c in pieces], width),
        out_shape=jax.ShapeDtypeStruct((tokens, cols), jnp.bfloat16),
        in_specs=[vmem] * (2 + len(pieces)),
        out_specs=vmem,
        compiler_params=pltpu.CompilerParams(vmem_limit_bytes=4 * MIB),
        cost_estimate=pl.CostEstimate(
            flops=tokens * cols, bytes_accessed=6 * tokens * cols, transcendentals=0
        ),
        name="combine",
    )(packet, other, *[a for a, _ in pieces])


def spread(own, packet, bits, blocks):
    width = own.shape[1]
    held, newest, other, last = {0: (own, 0)}, {}, None, None
    for bit in bits:
        arrived = {}
        if newest:
            for offset, (array, first) in held.items():
                if array.shape[1] != width:
                    array = array[:, first : first + width]
                arrived[offset ^ bit] = (swap(array, "row", bit), 0)
            packet = combine(packet, other, list(newest.values()), blocks, last, width)
        sent = list(newest) if newest else [0]
        other = swap(packet, "row", bit)
        held.update(newest)
        arrived |= {offset ^ bit: (other, i * width) for i, offset in enumerate(sent)}
        newest, last = arrived, bit
    held.update(newest)
    return held, {offset ^ last for offset in sent}, packet, other, last


def turn_kernel(tile, wq_hbm, wk_hbm, wv_hbm, *refs):
    out_ref, wq, wk, wv, sems = refs[-5:]
    steps = wq.shape[0] // tile
    copies = []
    for j in range(steps):
        rows = slice(j * tile, (j + 1) * tile)
        copies.append(
            [
                pltpu.make_async_copy(source.at[rows, :], target.at[rows, :], sems.at[j, i])
                for i, (source, target) in enumerate(
                    ((wq_hbm, wq), (wk_hbm, wk), (wv_hbm, wv))
                )
            ]
        )
        for copy in copies[j]:
            copy.start()
    for j in range(steps):
        rows = slice(j * tile, (j + 1) * tile)
        first = 0
        for copy, weight in zip(copies[j], (wq, wk, wv)):
            copy.wait()
            out_ref[first : first + weight.shape[1], rows] = weight[rows, :].T
            first += weight.shape[1]


def turn_weights(weights, after):
    features = weights[0].shape[0]
    widths = [w.shape[1] for w in weights]
    tile = min(512, features)
    hbm = pl.BlockSpec(memory_space=pltpu.HBM)
    return pl.pallas_call(
        functools.partial(turn_kernel, tile),
        out_shape=pltpu.VMEM((sum(widths), features), jnp.bfloat16),
        in_specs=[hbm] * 3 + [pl.BlockSpec(memory_space=pl.ANY)] * len(after),
        out_specs=pl.BlockSpec(memory_space=pltpu.VMEM),
        scratch_shapes=[pltpu.VMEM((features, width), jnp.bfloat16) for width in widths]
        + [pltpu.SemaphoreType.DMA((features // tile, 3))],
        compiler_params=pltpu.CompilerParams(vmem_limit_bytes=16 * MIB),
        cost_estimate=pl.CostEstimate(
            flops=0, bytes_accessed=4 * features * sum(widths), transcendentals=0
        ),
        name="turn_weights",
    )(*[pltpu.with_memory_space_constraint(w, pltpu.HBM) for w in weights], *after)


def early_kernel(columns, tile, *refs):
    count, width = len(columns[0]), refs[-1].shape[1] // 2
    w_ref, out_ref, gq = refs[2 * count :]
    tokens = refs[0].shape[0]
    for i in range(2):
        for k, first in enumerate(columns[i]):
            gq[k * tokens : (k + 1) * tokens, i * width : (i + 1) * width] = refs[
                i * count + k
            ][:, first : first + width]
    for j in range(w_ref.shape[1] // tile):
        cols = slice(j * tile, (j + 1) * tile)
        out_ref[:, cols] = contract(gq[...], w_ref[: 2 * width, cols], 1, 0).astype(
            jnp.bfloat16
        )


def early_product(pieces, blocks, width, weights):
    arrays = [side[b][0] for side in pieces for b in blocks]
    columns = [[side[b][1] for b in blocks] for side in pieces]
    tokens = arrays[0].shape[0]
    features = weights.shape[1]
    tile = min(1024, features)
    rows = len(blocks) * tokens
    vmem = pl.BlockSpec(memory_space=pltpu.VMEM)
    return pl.pallas_call(
        functools.partial(early_kernel, columns, tile),
        out_shape=jax.ShapeDtypeStruct((rows, features), jnp.bfloat16),
        in_specs=[vmem] * (len(arrays) + 1),
        out_specs=vmem,
        scratch_shapes=[pltpu.VMEM((rows, 2 * width), jnp.bfloat16)],
        compiler_params=pltpu.CompilerParams(vmem_limit_bytes=16 * MIB),
        cost_estimate=pl.CostEstimate(
            flops=4 * rows * features * width,
            bytes_accessed=4 * features * width + 2 * rows * features + 4 * rows * width,
            transcendentals=0,
        ),
        name="early_product",
    )(*arrays, weights)


def put_pair(target_ref, target, first, sums, offsets, blocks, b, start):
    count = target.stop - target.start
    if offsets is None:
        tokens = sums[0].shape[0] // blocks
        rows = pl.ds(pl.multiple_of(b * tokens + start, 16), count)
        target_ref[target, first:] = sums[0][rows, :]
        return
    rows = pl.ds(pl.multiple_of(start, 16), count)
    for i in range(2):
        cols = slice(first + i * HEAD_SIZE, first + (i + 1) * HEAD_SIZE)
        target_ref[target, cols] = summed_block(
            sums[2 * i], sums[2 * i + 1], blocks, b, offsets[i], rows
        )


def by_destination(blocks, half, place_ref, put):
    core, turn = place_ref[0], place_ref[1]
    for q in range(blocks):
        for b in range(blocks):

            @pl.when((q ^ turn) == b)
            def _():
                for side in range(2):
                    first = (side * blocks + q) * half
                    put(q, side, slice(first, first + half), b, (core ^ side) * half)


def last_kernel(early, late, columns, offsets, part, width, spare, place_ref, *refs):
    blocks = len(early) + len(late)
    early_ref, w_ref, refs = refs[0], refs[1], refs[2 + spare :]
    pieces = [refs[i * len(late) : (i + 1) * len(late)] for i in range(2)]
    refs = refs[2 * len(late) :]
    count = 1 if offsets is None else 4
    sums, refs = refs[:count], refs[count:]
    mine_refs, other_ref, gq, gkv, query, pair = refs[:blocks], *refs[blocks:]
    half = mine_refs[0].shape[0]
    tokens = 2 * half
    cols = slice(part * other_ref.shape[1], (part + 1) * other_ref.shape[1])

    for i in range(2):
        for k, first in enumerate(columns[i]):
            gq[k * tokens : (k + 1) * tokens, i * width : (i + 1) * width] = pieces[i][k][
                :, first : first + width
            ]

    def put_rows(q, side, target, b, start):
        put_pair(gkv, target, 0, sums, offsets, blocks, b, start)

    by_destination(blocks, half, place_ref, put_rows)
    query[...] = contract(gq[...], w_ref[: 2 * width, cols], 1, 0).astype(jnp.bfloat16)
    pair[...] = contract(gkv[...], w_ref[2 * width :, cols], 1, 0)

    def put_sum(q, side, target, b, start):
        if b in late:
            rows = pl.ds(pl.multiple_of(late.index(b) * tokens + start, 16), half)
            part_sum = query[rows, :]
        else:
            rows = pl.ds(pl.multiple_of(early.index(b) * tokens + start, 16), half)
            part_sum = early_ref[rows, cols]
        total = (pair[target, :] + part_sum.astype(jnp.float32)).astype(jnp.bfloat16)
        if side:
            other_ref[q * half : (q + 1) * half, :] = total
        else:
            mine_refs[q][...] = total

    by_destination(blocks, half, place_ref, put_sum)


def last_product(place, early, late, early_part, pieces, sums, offsets, weights, width, part, after):
    blocks = len(early) + len(late)
    arrays = [side[b][0] for side in pieces for b in late]
    columns = [[side[b][1] for b in late] for side in pieces]
    tokens = arrays[0].shape[0]
    half, cols = tokens // 2, weights.shape[1] // 2
    pair_cols = weights.shape[0] - 2 * width
    vmem = pl.BlockSpec(memory_space=pltpu.VMEM)
    *mine, other = pl.pallas_call(
        functools.partial(
            last_kernel, early, late, columns, offsets, part, width, len(after)
        ),
        out_shape=[jax.ShapeDtypeStruct((half, cols), jnp.bfloat16)] * blocks
        + [jax.ShapeDtypeStruct((blocks * half, cols), jnp.bfloat16)],
        in_specs=[pl.BlockSpec(memory_space=pltpu.SMEM)]
        + [vmem] * 2
        + [pl.BlockSpec(memory_space=pl.ANY)] * len(after)
        + [vmem] * (len(arrays) + len(sums)),
        out_specs=[vmem] * (blocks + 1),
        scratch_shapes=[
            pltpu.VMEM((len(late) * tokens, 2 * width), jnp.bfloat16),
            pltpu.VMEM((blocks * tokens, pair_cols), jnp.bfloat16),
            pltpu.VMEM((len(late) * tokens, cols), jnp.bfloat16),
            pltpu.VMEM((blocks * tokens, cols), jnp.float32),
        ],
        compiler_params=pltpu.CompilerParams(vmem_limit_bytes=16 * MIB),
        cost_estimate=pl.CostEstimate(
            flops=2 * tokens * cols * (len(late) * 2 * width + blocks * pair_cols),
            bytes_accessed=2 * cols * (2 * width + pair_cols) + 8 * blocks * tokens * cols,
            transcendentals=0,
        ),
        name="last_product",
    )(place, early_part, weights, *after, *arrays, *sums)
    return mine, other


def order_kernel(blocks, columns, offsets, width, place_ref, *refs):
    pieces = [refs[i * blocks : (i + 1) * blocks] for i in range(2)]
    sums, g = refs[2 * blocks : -2], refs[-1]
    half = g.shape[0] // (2 * blocks)

    def put(q, side, target, b, start):
        rows = pl.ds(pl.multiple_of(start, 16), half)
        for i in range(2):
            first = columns[i][b]
            g[target, i * width : (i + 1) * width] = pieces[i][b][rows, first : first + width]
        put_pair(g, target, 2 * width, sums, offsets, blocks, b, start)

    by_destination(blocks, half, place_ref, put)


def order_rows(place, pieces, sums, offsets, width, cols, after):
    blocks = len(pieces[0])
    arrays = [side[b][0] for side in pieces for b in range(blocks)]
    columns = [[side[b][1] for b in range(blocks)] for side in pieces]
    rows = blocks * arrays[0].shape[0]
    vmem = pl.BlockSpec(memory_space=pltpu.VMEM)
    return pl.pallas_call(
        functools.partial(order_kernel, blocks, columns, offsets, width),
        out_shape=jax.ShapeDtypeStruct((rows, cols), jnp.bfloat16),
        in_specs=[pl.BlockSpec(memory_space=pltpu.SMEM)]
        + [vmem] * (len(arrays) + len(sums))
        + [pl.BlockSpec(memory_space=pl.ANY)],
        out_specs=vmem,
        compiler_params=pltpu.CompilerParams(vmem_limit_bytes=8 * MIB),
        cost_estimate=pl.CostEstimate(
            flops=0, bytes_accessed=4 * rows * cols, transcendentals=0
        ),
        name="order_rows",
    )(place, *arrays, *sums, after)


def join_kernel(count, *refs):
    sources, out_ref, sems = refs[:count], refs[count + 1], refs[count + 2]
    rows = sources[0].shape[0]
    copies = [
        pltpu.make_async_copy(source, out_ref.at[i * rows : (i + 1) * rows, :], sems.at[i])
        for i, source in enumerate(sources)
    ]
    for copy in copies:
        copy.start()
    for copy in copies:
        copy.wait()


def join_rows(arrays, after):
    count = len(arrays)
    rows, cols = arrays[0].shape
    return pl.pallas_call(
        functools.partial(join_kernel, count),
        out_shape=jax.ShapeDtypeStruct((count * rows, cols), arrays[0].dtype),
        in_specs=[pl.BlockSpec(memory_space=pl.ANY)] * (count + 1),
        out_specs=pl.BlockSpec(memory_space=pltpu.VMEM),
        scratch_shapes=[pltpu.SemaphoreType.DMA((count,))],
        compiler_params=pltpu.CompilerParams(vmem_limit_bytes=4 * MIB),
        cost_estimate=pl.CostEstimate(
            flops=0, bytes_accessed=4 * count * rows * cols, transcendentals=0
        ),
        name="join_rows",
    )(*arrays, after)


def weight_grad_kernel(places, g_ref, *refs):
    pieces = len(places)
    x_refs = refs[:pieces]
    gwq_ref, gwk_ref, gwv_ref, x_all = refs[pieces:]
    query_cols, key_cols = gwq_ref.shape[1], gwk_ref.shape[1]
    rows = x_refs[0].shape[0]
    for place, x_ref in zip(places, x_refs):
        x_all[place * rows : (place + 1) * rows, :] = x_ref[...]
    x = x_all[...]
    gwq_ref[...] = contract(x, g_ref[:, :query_cols], 0, 0)
    pair = contract(x, g_ref[:, query_cols:], 0, 0)
    gwk_ref[...] = pair[:, :key_cols]
    gwv_ref[...] = pair[:, key_cols:]


def weight_grads(g, x_parts, order, query_cols):
    chips = len(order)
    features = x_parts[0].shape[1]
    piece_tokens = g.shape[0] // (2 * chips)
    places = [core * chips + q for core in range(2) for q in order]
    counts = [part.shape[0] // piece_tokens for part in x_parts]
    key_cols = (g.shape[1] - query_cols) // 2
    tile = min(256, features)
    return pl.pallas_call(
        functools.partial(weight_grad_kernel, places),
        grid=(features // tile,),
        out_shape=[
            jax.ShapeDtypeStruct((features, query_cols), jnp.float32),
            jax.ShapeDtypeStruct((features, key_cols), jnp.float32),
            jax.ShapeDtypeStruct((features, key_cols), jnp.float32),
        ],
        in_specs=[pl.BlockSpec(g.shape, lambda i: (0, 0))]
        + [
            pl.BlockSpec((piece_tokens, tile), lambda i, k=k: (k, i))
            for count in counts
            for k in range(count)
        ],
        out_specs=[
            pl.BlockSpec((tile, query_cols), lambda i: (i, 0)),
            pl.BlockSpec((tile, key_cols), lambda i: (i, 0)),
            pl.BlockSpec((tile, key_cols), lambda i: (i, 0)),
        ],
        scratch_shapes=[pltpu.VMEM((g.shape[0], tile), jnp.bfloat16)],
        compiler_params=pltpu.CompilerParams(vmem_limit_bytes=32 * MIB),
        cost_estimate=pl.CostEstimate(
            flops=2 * g.size * features,
            bytes_accessed=2 * g.size + 2 * g.shape[0] * features + 4 * features * g.shape[1],
            transcendentals=0,
        ),
        name="weight_grads",
    )(g, *[x for x, n in zip(x_parts, counts) for _ in range(n)])


def sum_kernel(count, groups, *refs):
    out_ref = refs[-1]
    for i in range(groups):
        cols = slice(
            i * out_ref.shape[1] // groups, (i + 1) * out_ref.shape[1] // groups
        )
        total = refs[i * count][...].astype(jnp.float32)
        for ref in refs[i * count + 1 : (i + 1) * count]:
            total += ref[...].astype(jnp.float32)
        for ref in refs[groups * count : -2]:
            total += ref[:, cols].astype(jnp.float32)
        out_ref[:, cols] = total.astype(out_ref.dtype)


def sum_rows(groups, whole, after):
    rows, cols = groups[0][0].shape
    terms = [term for group in groups for term in group] + whole
    vmem = pl.BlockSpec(memory_space=pltpu.VMEM)
    return pl.pallas_call(
        functools.partial(sum_kernel, len(groups[0]), len(groups)),
        out_shape=jax.ShapeDtypeStruct((rows, cols * len(groups)), jnp.bfloat16),
        in_specs=[vmem] * len(terms) + [pl.BlockSpec(memory_space=pl.ANY)],
        out_specs=vmem,
        compiler_params=pltpu.CompilerParams(vmem_limit_bytes=4 * MIB),
        cost_estimate=pl.CostEstimate(
            flops=len(terms) * rows * cols,
            bytes_accessed=4 * len(terms) * rows * cols,
            transcendentals=0,
        ),
        name="sum_rows",
    )(*terms, pltpu.with_memory_space_constraint(after, pltpu.HBM))


def shards(
    layer_input,
    w_query,
    w_key,
    w_value,
    rotated_query_state,
    rotated_key_state,
    saved_value_state,
    context_gradient,
    positions,
    segment_ids,
):
    tokens = rotated_query_state.shape[0]
    n_row, n_col = lax.axis_size("row"), lax.axis_size("col")
    chips = n_col // 2
    shared_heads = n_col // KEY_VALUE_HEADS
    row_index = lax.axis_index("row").astype(jnp.int32)
    col_index = lax.axis_index("col").astype(jnp.int32)
    chip_index, core_index = col_index // 2, col_index % 2

    key, value = rotated_key_state, saved_value_state
    if shared_heads > 1:
        pair = jnp.concatenate([key, value], axis=1)
        pair = [pair] + [swap(pair, "col", s) for s in range(1, shared_heads)]
        part = col_index % shared_heads
        stacked = jnp.stack(pair)
        stacked = jnp.take(stacked, jnp.arange(shared_heads) ^ part, axis=0)
        stacked = stacked.reshape(shared_heads, tokens, 2, -1).transpose(1, 2, 0, 3)
        stacked = stacked.reshape(tokens, 2, HEAD_SIZE)
        key, value = stacked[:, 0], stacked[:, 1]
    packed = gather_direct(pack(key, value, segment_ids), "row")

    row = row_index.reshape(1)
    query, out_grad, cosine, sine = prepare(
        row, n_row, rotated_query_state, context_gradient, positions, segment_ids
    )
    first, second, *packets = attention_backward(row, query, out_grad, packed, cosine, sine)
    bits = [1 << i for i in range(n_row.bit_length() - 1)]
    pieces, sums, offsets, late = [], [], [], set()
    for own, packet, order in zip((first, second), packets, (bits, bits[::-1])):
        held, with_last, *last_two, offset = spread(own, packet, order, n_row)
        pieces.append(held)
        late |= with_last
        sums += last_two
        offsets.append(offset)

    if shared_heads > 1:
        dkv = []
        for i in range(2):
            packet, other = (a[:, -n_row * HEAD_SIZE :] for a in sums[2 * i : 2 * i + 2])
            packet, other = (a.reshape(tokens, n_row, HEAD_SIZE) for a in (packet, other))
            dkv.append(add_low(packet, other[:, np.arange(n_row) ^ offsets[i]]))
        dkv = jnp.stack(dkv, axis=2)
        bit = shared_heads // 2
        while bit:
            half = dkv.shape[3] // 2
            upper = (col_index & bit) != 0
            lower_part, upper_part = dkv[..., :half], dkv[..., half:]
            kept = jnp.where(upper, upper_part, lower_part)
            sent = jnp.where(upper, lower_part, upper_part)
            dkv = add_low(kept, swap(sent, "col", bit))
            bit //= 2
        sums, offsets = [dkv.transpose(1, 0, 2, 3).reshape(n_row * tokens, -1)], None

    held, order = layer_input, [0]
    bit = chips // 2
    while bit > 1:
        held = join_rows([held, swap(held, "col", 2 * bit)], first)
        order += [q | bit for q in order]
        bit //= 2
    x_parts = [held, swap(held, "col", 2)]
    order += [q | 1 for q in order]

    place = jnp.stack([core_index, row_index ^ chip_index])
    weights = turn_weights((w_query, w_key, w_value), [sums[0]])
    weights = pltpu.with_memory_space_constraint(weights, pltpu.VMEM)
    width = first.shape[1]
    early = [b for b in range(n_row) if b not in late]
    late = sorted(late)
    early_part = early_product(pieces, early, width, weights)
    half = tokens // 2
    groups, after = [], x_parts
    for part in range(2):
        mine, other = last_product(
            place, early, late, early_part, pieces, sums, offsets, weights, width, part, after
        )
        after = mine[:1]
        other = swap(other, "col", 1)
        group = {
            q: add_low(mine[q], other[q * half : (q + 1) * half]) for q in range(chips)
        }
        groups.append(group)
    x_parts += [swap(part, "col", 1) for part in x_parts]
    cols = weights.shape[0]
    g = order_rows(place, pieces, sums, offsets, width, cols, groups[1][chips - 1])
    terms = [[group.pop(0)] for group in groups]
    whole = []
    bit = 1
    while bit < chips:
        for q in sorted((q for q in groups[0] if q & bit), reverse=True):
            sent = [group.pop(q) for group in groups]
            if q == bit and 2 * bit < chips:
                sent = jnp.concatenate(sent, axis=1)
                sent = lax.optimization_barrier((sent, received))[0]
                whole.append(swap(sent, "col", 2 * bit))
                continue
            for group, term, half_sent in zip(groups, terms, sent):
                received = swap(half_sent, "col", 2 * bit)
                if q == bit:
                    term.append(received)
                else:
                    group[q ^ bit] = add_low(group[q ^ bit], received)
        bit *= 2

    grad_wq, grad_wk, grad_wv = weight_grads(g, x_parts, order, w_query.shape[1])
    grad_input = sum_rows(terms, whole, grad_wk)
    return grad_input, grad_wq, grad_wk, grad_wv


def solution(mesh):
    return jax.shard_map(
        shards,
        mesh=mesh,
        in_specs=(
            P("col", "row"),
            P("row", "col"),
            P("row", "col"),
            P("row", "col"),
            P("row", "col"),
            P("row", "col"),
            P("row", "col"),
            P("row", "col"),
            P("row"),
            P("row"),
        ),
        out_specs=(P("col", "row"), P("row", "col"), P("row", "col"), P("row", "col")),
        check_vma=False,
    )
```

```python
import functools
import math

import jax
import jax.numpy as jnp
import numpy as np
from jax import lax
from jax.experimental import pallas as pl
from jax.experimental.pallas import tpu as pltpu
from jax.sharding import PartitionSpec as P

KEY_VALUE_HEADS = 8
HEAD_SIZE = 128
ROPE_BASE = 500000.0
PAD_ROWS = 16
MIB = 1024 * 1024


def contract(left, right, left_dim, right_dim):
    return lax.dot_general(
        left, right, (((left_dim,), (right_dim,)), ((), ())), preferred_element_type=jnp.float32
    )


def swap(value, axis, offset):
    pairs = [(source, source ^ offset) for source in range(lax.axis_size(axis))]
    return lax.ppermute(value, axis, pairs)


def gather_direct(value, axis):
    return [value] + [swap(value, axis, s) for s in range(1, lax.axis_size(axis))]


def add_low(left, right):
    return (left.astype(jnp.float32) + right.astype(jnp.float32)).astype(jnp.bfloat16)


def block_index(position, row, blocks, tokens):
    index = position
    for b in range(blocks):
        index = jnp.where(position >= b * tokens, position + ((row ^ b) - b) * tokens, index)
    return index.astype(jnp.float32)


def unrotate(gradient, cosine, sine):
    return gradient * cosine + pltpu.roll(gradient, HEAD_SIZE // 2, 1) * sine


def pack_kernel(k_ref, v_ref, ids_ref, out_ref):
    tokens = k_ref.shape[0]
    out_ref[:tokens, :HEAD_SIZE] = k_ref[...]
    out_ref[:tokens, HEAD_SIZE:] = v_ref[...]
    width = ids_ref.shape[1]
    row = lax.broadcasted_iota(jnp.int32, (PAD_ROWS, width), 0)
    ids = jnp.ones((PAD_ROWS, width), jnp.float32)
    for i in range(ids_ref.shape[0]):
        ids = jnp.where(row == i, ids_ref[i : i + 1, :].astype(jnp.float32), ids)
    out_ref[tokens:, :] = jnp.ones((PAD_ROWS, out_ref.shape[1]), jnp.bfloat16)
    out_ref[tokens:, :width] = ids.astype(jnp.bfloat16)


def pack(key, value, segment_ids):
    tokens = key.shape[0]
    width = 2 * HEAD_SIZE
    rows = -(-tokens // width)
    ids = segment_ids
    if rows > 1:
        ids = jnp.pad(ids, (0, rows * width - tokens), constant_values=1)
    ids = ids.reshape(rows, -1)
    vmem = pl.BlockSpec(memory_space=pltpu.VMEM)
    return pl.pallas_call(
        pack_kernel,
        out_shape=jax.ShapeDtypeStruct((tokens + PAD_ROWS, width), jnp.bfloat16),
        in_specs=[vmem] * 3,
        out_specs=vmem,
        compiler_params=pltpu.CompilerParams(vmem_limit_bytes=MIB),
        cost_estimate=pl.CostEstimate(
            flops=0, bytes_accessed=8 * tokens * HEAD_SIZE, transcendentals=0
        ),
        name="pack",
    )(
        pltpu.with_memory_space_constraint(key, pltpu.HBM),
        pltpu.with_memory_space_constraint(value, pltpu.HBM),
        pltpu.with_memory_space_constraint(ids, pltpu.HBM),
    )


def prepare_kernel(heads, blocks, row_ref, q_hbm, o_hbm, positions_ref, ids_ref, freq_ref, *refs):
    q_ref, o_ref, cos_ref, sin_ref, sems = refs
    tokens = q_hbm.shape[0]
    row = row_ref[0]
    copies = []
    for h in range(heads):
        rows = slice(h * tokens, (h + 1) * tokens)
        cols = slice(h * HEAD_SIZE, (h + 1) * HEAD_SIZE)
        for i, (source, target) in enumerate(((q_hbm, q_ref), (o_hbm, o_ref))):
            copies.append(
                pltpu.make_async_copy(source.at[:, cols], target.at[rows, :], sems.at[h, i])
            )
            copies[-1].start()

    first = (row * tokens).astype(jnp.float32)
    last = first + (tokens - 1)
    positions = positions_ref[...].astype(jnp.float32)
    cut = first + jnp.sum(1.0 - ids_ref[...].astype(jnp.float32), axis=1, keepdims=True)
    offset_low = positions[:, :1] - first
    offset_high = positions[:, tokens - 1 :] - last
    place = lax.broadcasted_iota(jnp.int32, (blocks * tokens, 1), 0)
    index = block_index(place, row, blocks, tokens)
    angle = (index + jnp.where(index < cut, offset_low, offset_high)) * freq_ref[...]
    lane = lax.broadcasted_iota(jnp.int32, (1, HEAD_SIZE), 1)
    lower = lane < HEAD_SIZE // 2
    table = jnp.cos(angle - jnp.where(lower, 0.0, math.pi / 2))
    turned = pltpu.roll(table, HEAD_SIZE // 2, 1)
    cos_ref[...] = jnp.where(lower, table, turned)
    sin_ref[...] = jnp.where(lower, turned, -table)

    for copy in copies:
        copy.wait()


def prepare(row, blocks, query, out_grad, positions, segment_ids):
    tokens, width = query.shape
    heads = width // HEAD_SIZE
    half_width = HEAD_SIZE // 2
    freq = np.exp(-(2.0 * np.arange(half_width) / HEAD_SIZE) * math.log(ROPE_BASE))
    freq = np.tile(freq, 2)[None].astype(np.float32)
    vmem = pl.BlockSpec(memory_space=pltpu.VMEM)
    hbm = pl.BlockSpec(memory_space=pltpu.HBM)
    return pl.pallas_call(
        functools.partial(prepare_kernel, heads, blocks),
        out_shape=[jax.ShapeDtypeStruct((heads * tokens, HEAD_SIZE), jnp.bfloat16)] * 2
        + [jax.ShapeDtypeStruct((blocks * tokens, HEAD_SIZE), jnp.float32)] * 2,
        in_specs=[pl.BlockSpec(memory_space=pltpu.SMEM), hbm, hbm, vmem, vmem, vmem],
        out_specs=[vmem] * 4,
        scratch_shapes=[pltpu.SemaphoreType.DMA((heads, 2))],
        compiler_params=pltpu.CompilerParams(vmem_limit_bytes=8 * MIB),
        cost_estimate=pl.CostEstimate(
            flops=0,
            bytes_accessed=8 * tokens * width,
            transcendentals=2 * blocks * tokens * HEAD_SIZE,
        ),
        name="prepare",
    )(
        row,
        pltpu.with_memory_space_constraint(query, pltpu.HBM),
        pltpu.with_memory_space_constraint(out_grad, pltpu.HBM),
        pltpu.with_memory_space_constraint(positions.reshape(1, -1), pltpu.HBM),
        pltpu.with_memory_space_constraint(segment_ids.reshape(1, -1), pltpu.HBM),
        pltpu.with_memory_space_constraint(jnp.asarray(freq), pltpu.HBM),
    )


def attention_kernel(heads, blocks, row_ref, q_all, o_all, *refs):
    kv_refs = refs[:blocks]
    cos_ref, sin_ref = refs[blocks : blocks + 2]
    dq_refs, packet_refs = refs[blocks + 2 : blocks + 4], refs[blocks + 4 : blocks + 6]
    k_all, v_all, ds_all, w_all, bias_ref, scores_ref, dweights_ref = refs[blocks + 6 :]
    together = scores_ref.shape[0] // bias_ref.shape[0]
    tokens = q_all.shape[0] // heads
    width = dq_refs[0].shape[1]
    keys = tokens * blocks
    scale = HEAD_SIZE**-0.5
    row = row_ref[0]

    cut = jnp.zeros((1, 1), jnp.float32)
    for b in range(blocks):
        rows = slice(b * tokens, (b + 1) * tokens)
        k_all[rows, :] = kv_refs[b][:tokens, :HEAD_SIZE]
        v_all[rows, :] = kv_refs[b][:tokens, HEAD_SIZE:]
        first = 1.0 - kv_refs[b][tokens:, :].astype(jnp.float32)
        cut += jnp.sum(jnp.sum(first, axis=0, keepdims=True), axis=1, keepdims=True)
    lane = lax.broadcasted_iota(jnp.int32, (1, keys), 1)
    key_index = block_index(lane, row, blocks, tokens)
    query_index = (
        lax.broadcasted_iota(jnp.int32, (tokens, 1), 0) + row * tokens
    ).astype(jnp.float32)
    lowest = jnp.where(query_index < cut, 0.0, cut)
    visible = (key_index <= query_index) & (key_index >= lowest)
    bias_ref[...] = jnp.where(visible, 0.0, -1e30)

    for h in range(heads):
        if h % together == 0:
            rows = slice(h * tokens, (h + together) * tokens)
            scores_ref[...] = contract(q_all[rows, :], k_all[...], 1, 1)
            dweights_ref[...] = contract(o_all[rows, :], v_all[...], 1, 1)
        rows = slice(h % together * tokens, (h % together + 1) * tokens)
        scores = scores_ref[rows, :] + bias_ref[...]
        peak = jnp.max(scores, axis=1, keepdims=True)
        terms = jnp.exp2((scores - peak) * (scale * math.log2(math.e)))
        inverse = 1.0 / jnp.sum(terms, axis=1, keepdims=True)
        dweights = dweights_ref[rows, :]
        weights = terms * inverse
        delta = jnp.sum(weights * dweights, axis=1, keepdims=True)
        dscores = (weights * (dweights - delta) * scale).astype(jnp.bfloat16)
        rows = slice(h * tokens, (h + 1) * tokens)
        w_all[rows, :] = weights.astype(jnp.bfloat16)
        ds_all[rows, :] = dscores
    dq = contract(ds_all[...], k_all[...], 1, 0)
    for h in range(heads):
        side, first = divmod(h * HEAD_SIZE, width)
        cols = slice(first, first + HEAD_SIZE)
        head = dq[h * tokens : (h + 1) * tokens]
        head = unrotate(head, cos_ref[:tokens, :], sin_ref[:tokens, :]).astype(jnp.bfloat16)
        dq_refs[side][:, cols] = head
        packet_refs[side][:, cols] = head
    dk = contract(ds_all[...], q_all[...], 0, 0)
    dk = unrotate(dk, cos_ref[...], sin_ref[...]).astype(jnp.bfloat16)
    dv = contract(w_all[...], o_all[...], 0, 0).astype(jnp.bfloat16)
    for b in range(blocks):
        rows = slice(b * tokens, (b + 1) * tokens)
        cols = slice(width + b * HEAD_SIZE, width + (b + 1) * HEAD_SIZE)
        packet_refs[0][:, cols] = dk[rows]
        packet_refs[1][:, cols] = dv[rows]


def attention_backward(row, query, out_grad, packed, cosine, sine):
    blocks = len(packed)
    keys = cosine.shape[0]
    tokens = keys // blocks
    heads = query.shape[0] // tokens
    width = heads // 2 * HEAD_SIZE
    vmem = pl.BlockSpec(memory_space=pltpu.VMEM)
    return pl.pallas_call(
        functools.partial(attention_kernel, heads, blocks),
        out_shape=[jax.ShapeDtypeStruct((tokens, width), jnp.bfloat16)] * 2
        + [jax.ShapeDtypeStruct((tokens, width + blocks * HEAD_SIZE), jnp.bfloat16)] * 2,
        in_specs=[pl.BlockSpec(memory_space=pltpu.SMEM)] + [vmem] * (blocks + 4),
        out_specs=[vmem] * 4,
        scratch_shapes=[
            pltpu.VMEM((keys, HEAD_SIZE), jnp.bfloat16),
            pltpu.VMEM((keys, HEAD_SIZE), jnp.bfloat16),
            pltpu.VMEM((heads * tokens, keys), jnp.bfloat16),
            pltpu.VMEM((heads * tokens, keys), jnp.bfloat16),
            pltpu.VMEM((tokens, keys), jnp.float32),
            pltpu.VMEM((min(4, heads) * tokens, keys), jnp.float32),
            pltpu.VMEM((min(4, heads) * tokens, keys), jnp.float32),
        ],
        compiler_params=pltpu.CompilerParams(vmem_limit_bytes=32 * MIB),
        cost_estimate=pl.CostEstimate(
            flops=10 * heads * tokens * keys * HEAD_SIZE,
            bytes_accessed=16 * tokens * width + 16 * keys * HEAD_SIZE,
            transcendentals=heads * tokens * keys,
        ),
        name="attention_backward",
    )(row, query, out_grad, *packed, cosine, sine)


def combine_kernel(blocks, offset, columns, width, *refs):
    packet_ref, other_ref, out_ref = refs[0], refs[1], refs[-1]
    for i, first in enumerate(columns):
        out_ref[:, i * width : (i + 1) * width] = refs[2 + i][:, first : first + width]
    for b in range(blocks):
        first = len(columns) * width + b * HEAD_SIZE
        out_ref[:, first : first + HEAD_SIZE] = summed_block(
            packet_ref, other_ref, blocks, b, offset, slice(None)
        )


def summed_block(packet_ref, other_ref, blocks, b, offset, rows):
    first = packet_ref.shape[1] - (blocks - b) * HEAD_SIZE
    total = packet_ref[rows, first : first + HEAD_SIZE].astype(jnp.float32)
    first = other_ref.shape[1] - (blocks - (b ^ offset)) * HEAD_SIZE
    total += other_ref[rows, first : first + HEAD_SIZE].astype(jnp.float32)
    return total.astype(jnp.bfloat16)


def combine(packet, other, pieces, blocks, offset, width):
    tokens = packet.shape[0]
    cols = len(pieces) * width + blocks * HEAD_SIZE
    vmem = pl.BlockSpec(memory_space=pltpu.VMEM)
    return pl.pallas_call(
        functools.partial(combine_kernel, blocks, offset, [c for _, c in pieces], width),
        out_shape=jax.ShapeDtypeStruct((tokens, cols), jnp.bfloat16),
        in_specs=[vmem] * (2 + len(pieces)),
        out_specs=vmem,
        compiler_params=pltpu.CompilerParams(vmem_limit_bytes=4 * MIB),
        cost_estimate=pl.CostEstimate(
            flops=tokens * cols, bytes_accessed=6 * tokens * cols, transcendentals=0
        ),
        name="combine",
    )(packet, other, *[a for a, _ in pieces])


def spread(own, packet, bits, blocks):
    width = own.shape[1]
    held, newest, other, last = {0: (own, 0)}, {}, None, None
    for bit in bits:
        arrived = {}
        if newest:
            for offset, (array, first) in held.items():
                if array.shape[1] != width:
                    array = array[:, first : first + width]
                arrived[offset ^ bit] = (swap(array, "row", bit), 0)
            packet = combine(packet, other, list(newest.values()), blocks, last, width)
        sent = list(newest) if newest else [0]
        other = swap(packet, "row", bit)
        held.update(newest)
        arrived |= {offset ^ bit: (other, i * width) for i, offset in enumerate(sent)}
        newest, last = arrived, bit
    held.update(newest)
    return held, {offset ^ last for offset in sent}, packet, other, last


def turn_kernel(tile, wq_hbm, wk_hbm, wv_hbm, *refs):
    out_ref, wq, wk, wv, sems = refs[-5:]
    steps = wq.shape[0] // tile
    copies = []
    for j in range(steps):
        rows = slice(j * tile, (j + 1) * tile)
        copies.append(
            [
                pltpu.make_async_copy(source.at[rows, :], target.at[rows, :], sems.at[j, i])
                for i, (source, target) in enumerate(
                    ((wq_hbm, wq), (wk_hbm, wk), (wv_hbm, wv))
                )
            ]
        )
        for copy in copies[j]:
            copy.start()
    for j in range(steps):
        rows = slice(j * tile, (j + 1) * tile)
        first = 0
        for copy, weight in zip(copies[j], (wq, wk, wv)):
            copy.wait()
            out_ref[first : first + weight.shape[1], rows] = weight[rows, :].T
            first += weight.shape[1]


def turn_weights(weights, after):
    features = weights[0].shape[0]
    widths = [w.shape[1] for w in weights]
    tile = min(512, features)
    hbm = pl.BlockSpec(memory_space=pltpu.HBM)
    return pl.pallas_call(
        functools.partial(turn_kernel, tile),
        out_shape=pltpu.VMEM((sum(widths), features), jnp.bfloat16),
        in_specs=[hbm] * 3 + [pl.BlockSpec(memory_space=pl.ANY)] * len(after),
        out_specs=pl.BlockSpec(memory_space=pltpu.VMEM),
        scratch_shapes=[pltpu.VMEM((features, width), jnp.bfloat16) for width in widths]
        + [pltpu.SemaphoreType.DMA((features // tile, 3))],
        compiler_params=pltpu.CompilerParams(vmem_limit_bytes=16 * MIB),
        cost_estimate=pl.CostEstimate(
            flops=0, bytes_accessed=4 * features * sum(widths), transcendentals=0
        ),
        name="turn_weights",
    )(*[pltpu.with_memory_space_constraint(w, pltpu.HBM) for w in weights], *after)


def early_kernel(columns, tile, *refs):
    count, width = len(columns[0]), refs[-1].shape[1] // 2
    w_ref, out_ref, gq = refs[2 * count :]
    tokens = refs[0].shape[0]
    for i in range(2):
        for k, first in enumerate(columns[i]):
            gq[k * tokens : (k + 1) * tokens, i * width : (i + 1) * width] = refs[
                i * count + k
            ][:, first : first + width]
    for j in range(w_ref.shape[1] // tile):
        cols = slice(j * tile, (j + 1) * tile)
        out_ref[:, cols] = contract(gq[...], w_ref[: 2 * width, cols], 1, 0).astype(
            jnp.bfloat16
        )


def early_product(pieces, blocks, width, weights):
    arrays = [side[b][0] for side in pieces for b in blocks]
    columns = [[side[b][1] for b in blocks] for side in pieces]
    tokens = arrays[0].shape[0]
    features = weights.shape[1]
    tile = min(1024, features)
    rows = len(blocks) * tokens
    vmem = pl.BlockSpec(memory_space=pltpu.VMEM)
    return pl.pallas_call(
        functools.partial(early_kernel, columns, tile),
        out_shape=jax.ShapeDtypeStruct((rows, features), jnp.bfloat16),
        in_specs=[vmem] * (len(arrays) + 1),
        out_specs=vmem,
        scratch_shapes=[pltpu.VMEM((rows, 2 * width), jnp.bfloat16)],
        compiler_params=pltpu.CompilerParams(vmem_limit_bytes=16 * MIB),
        cost_estimate=pl.CostEstimate(
            flops=4 * rows * features * width,
            bytes_accessed=4 * features * width + 2 * rows * features + 4 * rows * width,
            transcendentals=0,
        ),
        name="early_product",
    )(*arrays, weights)


def put_pair(target_ref, target, first, sums, offsets, blocks, b, start):
    count = target.stop - target.start
    if offsets is None:
        tokens = sums[0].shape[0] // blocks
        rows = pl.ds(pl.multiple_of(b * tokens + start, 16), count)
        target_ref[target, first:] = sums[0][rows, :]
        return
    rows = pl.ds(pl.multiple_of(start, 16), count)
    for i in range(2):
        cols = slice(first + i * HEAD_SIZE, first + (i + 1) * HEAD_SIZE)
        target_ref[target, cols] = summed_block(
            sums[2 * i], sums[2 * i + 1], blocks, b, offsets[i], rows
        )


def by_destination(blocks, half, place_ref, put):
    core, turn = place_ref[0], place_ref[1]
    for q in range(blocks):
        for b in range(blocks):

            @pl.when((q ^ turn) == b)
            def _():
                for side in range(2):
                    first = (side * blocks + q) * half
                    put(q, side, slice(first, first + half), b, (core ^ side) * half)


def last_kernel(early, late, columns, offsets, part, width, spare, place_ref, *refs):
    blocks = len(early) + len(late)
    early_ref, w_ref, refs = refs[0], refs[1], refs[2 + spare :]
    pieces = [refs[i * len(late) : (i + 1) * len(late)] for i in range(2)]
    refs = refs[2 * len(late) :]
    count = 1 if offsets is None else 4
    sums, refs = refs[:count], refs[count:]
    mine_refs, other_ref, gq, gkv, query, pair = refs[:blocks], *refs[blocks:]
    half = mine_refs[0].shape[0]
    tokens = 2 * half
    cols = slice(part * other_ref.shape[1], (part + 1) * other_ref.shape[1])

    for i in range(2):
        for k, first in enumerate(columns[i]):
            gq[k * tokens : (k + 1) * tokens, i * width : (i + 1) * width] = pieces[i][k][
                :, first : first + width
            ]

    def put_rows(q, side, target, b, start):
        put_pair(gkv, target, 0, sums, offsets, blocks, b, start)

    by_destination(blocks, half, place_ref, put_rows)
    query[...] = contract(gq[...], w_ref[: 2 * width, cols], 1, 0).astype(jnp.bfloat16)
    pair[...] = contract(gkv[...], w_ref[2 * width :, cols], 1, 0)

    def put_sum(q, side, target, b, start):
        if b in late:
            rows = pl.ds(pl.multiple_of(late.index(b) * tokens + start, 16), half)
            part_sum = query[rows, :]
        else:
            rows = pl.ds(pl.multiple_of(early.index(b) * tokens + start, 16), half)
            part_sum = early_ref[rows, cols]
        total = (pair[target, :] + part_sum.astype(jnp.float32)).astype(jnp.bfloat16)
        if side:
            other_ref[q * half : (q + 1) * half, :] = total
        else:
            mine_refs[q][...] = total

    by_destination(blocks, half, place_ref, put_sum)


def last_product(place, early, late, early_part, pieces, sums, offsets, weights, width, part, after):
    blocks = len(early) + len(late)
    arrays = [side[b][0] for side in pieces for b in late]
    columns = [[side[b][1] for b in late] for side in pieces]
    tokens = arrays[0].shape[0]
    half, cols = tokens // 2, weights.shape[1] // 2
    pair_cols = weights.shape[0] - 2 * width
    vmem = pl.BlockSpec(memory_space=pltpu.VMEM)
    *mine, other = pl.pallas_call(
        functools.partial(
            last_kernel, early, late, columns, offsets, part, width, len(after)
        ),
        out_shape=[jax.ShapeDtypeStruct((half, cols), jnp.bfloat16)] * blocks
        + [jax.ShapeDtypeStruct((blocks * half, cols), jnp.bfloat16)],
        in_specs=[pl.BlockSpec(memory_space=pltpu.SMEM)]
        + [vmem] * 2
        + [pl.BlockSpec(memory_space=pl.ANY)] * len(after)
        + [vmem] * (len(arrays) + len(sums)),
        out_specs=[vmem] * (blocks + 1),
        scratch_shapes=[
            pltpu.VMEM((len(late) * tokens, 2 * width), jnp.bfloat16),
            pltpu.VMEM((blocks * tokens, pair_cols), jnp.bfloat16),
            pltpu.VMEM((len(late) * tokens, cols), jnp.bfloat16),
            pltpu.VMEM((blocks * tokens, cols), jnp.float32),
        ],
        compiler_params=pltpu.CompilerParams(vmem_limit_bytes=16 * MIB),
        cost_estimate=pl.CostEstimate(
            flops=2 * tokens * cols * (len(late) * 2 * width + blocks * pair_cols),
            bytes_accessed=2 * cols * (2 * width + pair_cols) + 8 * blocks * tokens * cols,
            transcendentals=0,
        ),
        name="last_product",
    )(place, early_part, weights, *after, *arrays, *sums)
    return mine, other


def order_kernel(blocks, columns, offsets, width, place_ref, *refs):
    pieces = [refs[i * blocks : (i + 1) * blocks] for i in range(2)]
    sums, g = refs[2 * blocks : -2], refs[-1]
    half = g.shape[0] // (2 * blocks)

    def put(q, side, target, b, start):
        rows = pl.ds(pl.multiple_of(start, 16), half)
        for i in range(2):
            first = columns[i][b]
            g[target, i * width : (i + 1) * width] = pieces[i][b][rows, first : first + width]
        put_pair(g, target, 2 * width, sums, offsets, blocks, b, start)

    by_destination(blocks, half, place_ref, put)


def order_rows(place, pieces, sums, offsets, width, cols, after):
    blocks = len(pieces[0])
    arrays = [side[b][0] for side in pieces for b in range(blocks)]
    columns = [[side[b][1] for b in range(blocks)] for side in pieces]
    rows = blocks * arrays[0].shape[0]
    vmem = pl.BlockSpec(memory_space=pltpu.VMEM)
    return pl.pallas_call(
        functools.partial(order_kernel, blocks, columns, offsets, width),
        out_shape=jax.ShapeDtypeStruct((rows, cols), jnp.bfloat16),
        in_specs=[pl.BlockSpec(memory_space=pltpu.SMEM)]
        + [vmem] * (len(arrays) + len(sums))
        + [pl.BlockSpec(memory_space=pl.ANY)],
        out_specs=vmem,
        compiler_params=pltpu.CompilerParams(vmem_limit_bytes=8 * MIB),
        cost_estimate=pl.CostEstimate(
            flops=0, bytes_accessed=4 * rows * cols, transcendentals=0
        ),
        name="order_rows",
    )(place, *arrays, *sums, after)


def join_kernel(count, *refs):
    sources, out_ref, sems = refs[:count], refs[count + 1], refs[count + 2]
    rows = sources[0].shape[0]
    copies = [
        pltpu.make_async_copy(source, out_ref.at[i * rows : (i + 1) * rows, :], sems.at[i])
        for i, source in enumerate(sources)
    ]
    for copy in copies:
        copy.start()
    for copy in copies:
        copy.wait()


def join_rows(arrays, after):
    count = len(arrays)
    rows, cols = arrays[0].shape
    return pl.pallas_call(
        functools.partial(join_kernel, count),
        out_shape=jax.ShapeDtypeStruct((count * rows, cols), arrays[0].dtype),
        in_specs=[pl.BlockSpec(memory_space=pl.ANY)] * (count + 1),
        out_specs=pl.BlockSpec(memory_space=pltpu.VMEM),
        scratch_shapes=[pltpu.SemaphoreType.DMA((count,))],
        compiler_params=pltpu.CompilerParams(vmem_limit_bytes=4 * MIB),
        cost_estimate=pl.CostEstimate(
            flops=0, bytes_accessed=4 * count * rows * cols, transcendentals=0
        ),
        name="join_rows",
    )(*arrays, after)


def weight_grad_kernel(places, g_ref, *refs):
    pieces = len(places)
    x_refs = refs[:pieces]
    gwq_ref, gwk_ref, gwv_ref, x_all = refs[pieces:]
    query_cols, key_cols = gwq_ref.shape[1], gwk_ref.shape[1]
    rows = x_refs[0].shape[0]
    for place, x_ref in zip(places, x_refs):
        x_all[place * rows : (place + 1) * rows, :] = x_ref[...]
    x = x_all[...]
    gwq_ref[...] = contract(x, g_ref[:, :query_cols], 0, 0)
    pair = contract(x, g_ref[:, query_cols:], 0, 0)
    gwk_ref[...] = pair[:, :key_cols]
    gwv_ref[...] = pair[:, key_cols:]


def weight_grads(g, x_parts, order, query_cols):
    chips = len(order)
    features = x_parts[0].shape[1]
    piece_tokens = g.shape[0] // (2 * chips)
    places = [core * chips + q for core in range(2) for q in order]
    counts = [part.shape[0] // piece_tokens for part in x_parts]
    key_cols = (g.shape[1] - query_cols) // 2
    tile = min(256, features)
    return pl.pallas_call(
        functools.partial(weight_grad_kernel, places),
        grid=(features // tile,),
        out_shape=[
            jax.ShapeDtypeStruct((features, query_cols), jnp.float32),
            jax.ShapeDtypeStruct((features, key_cols), jnp.float32),
            jax.ShapeDtypeStruct((features, key_cols), jnp.float32),
        ],
        in_specs=[pl.BlockSpec(g.shape, lambda i: (0, 0))]
        + [
            pl.BlockSpec((piece_tokens, tile), lambda i, k=k: (k, i))
            for count in counts
            for k in range(count)
        ],
        out_specs=[
            pl.BlockSpec((tile, query_cols), lambda i: (i, 0)),
            pl.BlockSpec((tile, key_cols), lambda i: (i, 0)),
            pl.BlockSpec((tile, key_cols), lambda i: (i, 0)),
        ],
        scratch_shapes=[pltpu.VMEM((g.shape[0], tile), jnp.bfloat16)],
        compiler_params=pltpu.CompilerParams(vmem_limit_bytes=32 * MIB),
        cost_estimate=pl.CostEstimate(
            flops=2 * g.size * features,
            bytes_accessed=2 * g.size + 2 * g.shape[0] * features + 4 * features * g.shape[1],
            transcendentals=0,
        ),
        name="weight_grads",
    )(g, *[x for x, n in zip(x_parts, counts) for _ in range(n)])


def sum_kernel(count, groups, *refs):
    out_ref = refs[-1]
    for i in range(groups):
        cols = slice(
            i * out_ref.shape[1] // groups, (i + 1) * out_ref.shape[1] // groups
        )
        total = refs[i * count][...].astype(jnp.float32)
        for ref in refs[i * count + 1 : (i + 1) * count]:
            total += ref[...].astype(jnp.float32)
        for ref in refs[groups * count : -2]:
            total += ref[:, cols].astype(jnp.float32)
        out_ref[:, cols] = total.astype(out_ref.dtype)


def sum_rows(groups, whole, after):
    rows, cols = groups[0][0].shape
    terms = [term for group in groups for term in group] + whole
    vmem = pl.BlockSpec(memory_space=pltpu.VMEM)
    return pl.pallas_call(
        functools.partial(sum_kernel, len(groups[0]), len(groups)),
        out_shape=jax.ShapeDtypeStruct((rows, cols * len(groups)), jnp.bfloat16),
        in_specs=[vmem] * len(terms) + [pl.BlockSpec(memory_space=pl.ANY)],
        out_specs=vmem,
        compiler_params=pltpu.CompilerParams(vmem_limit_bytes=4 * MIB),
        cost_estimate=pl.CostEstimate(
            flops=len(terms) * rows * cols,
            bytes_accessed=4 * len(terms) * rows * cols,
            transcendentals=0,
        ),
        name="sum_rows",
    )(*terms, pltpu.with_memory_space_constraint(after, pltpu.HBM))


def shards(
    layer_input,
    w_query,
    w_key,
    w_value,
    rotated_query_state,
    rotated_key_state,
    saved_value_state,
    context_gradient,
    positions,
    segment_ids,
):
    tokens = rotated_query_state.shape[0]
    n_row, n_col = lax.axis_size("row"), lax.axis_size("col")
    chips = n_col // 2
    shared_heads = n_col // KEY_VALUE_HEADS
    row_index = lax.axis_index("row").astype(jnp.int32)
    col_index = lax.axis_index("col").astype(jnp.int32)
    chip_index, core_index = col_index // 2, col_index % 2

    key, value = rotated_key_state, saved_value_state
    if shared_heads > 1:
        pair = jnp.concatenate([key, value], axis=1)
        pair = [pair] + [swap(pair, "col", s) for s in range(1, shared_heads)]
        part = col_index % shared_heads
        stacked = jnp.stack(pair)
        stacked = jnp.take(stacked, jnp.arange(shared_heads) ^ part, axis=0)
        stacked = stacked.reshape(shared_heads, tokens, 2, -1).transpose(1, 2, 0, 3)
        stacked = stacked.reshape(tokens, 2, HEAD_SIZE)
        key, value = stacked[:, 0], stacked[:, 1]
    packed = gather_direct(pack(key, value, segment_ids), "row")

    row = row_index.reshape(1)
    query, out_grad, cosine, sine = prepare(
        row, n_row, rotated_query_state, context_gradient, positions, segment_ids
    )
    first, second, *packets = attention_backward(row, query, out_grad, packed, cosine, sine)
    bits = [1 << i for i in range(n_row.bit_length() - 1)]
    pieces, sums, offsets, late = [], [], [], set()
    for own, packet, order in zip((first, second), packets, (bits, bits[::-1])):
        held, with_last, *last_two, offset = spread(own, packet, order, n_row)
        pieces.append(held)
        late |= with_last
        sums += last_two
        offsets.append(offset)

    if shared_heads > 1:
        dkv = []
        for i in range(2):
            packet, other = (a[:, -n_row * HEAD_SIZE :] for a in sums[2 * i : 2 * i + 2])
            packet, other = (a.reshape(tokens, n_row, HEAD_SIZE) for a in (packet, other))
            dkv.append(add_low(packet, other[:, np.arange(n_row) ^ offsets[i]]))
        dkv = jnp.stack(dkv, axis=2)
        bit = shared_heads // 2
        while bit:
            half = dkv.shape[3] // 2
            upper = (col_index & bit) != 0
            lower_part, upper_part = dkv[..., :half], dkv[..., half:]
            kept = jnp.where(upper, upper_part, lower_part)
            sent = jnp.where(upper, lower_part, upper_part)
            dkv = add_low(kept, swap(sent, "col", bit))
            bit //= 2
        sums, offsets = [dkv.transpose(1, 0, 2, 3).reshape(n_row * tokens, -1)], None

    held, order = layer_input, [0]
    bit = chips // 2
    while bit > 1:
        held = join_rows([held, swap(held, "col", 2 * bit)], first)
        order += [q | bit for q in order]
        bit //= 2
    x_parts = [held, swap(held, "col", 2)]
    order += [q | 1 for q in order]

    place = jnp.stack([core_index, row_index ^ chip_index])
    weights = turn_weights((w_query, w_key, w_value), [sums[0]])
    weights = pltpu.with_memory_space_constraint(weights, pltpu.VMEM)
    width = first.shape[1]
    early = [b for b in range(n_row) if b not in late]
    late = sorted(late)
    early_part = early_product(pieces, early, width, weights)
    half = tokens // 2
    groups, after = [], x_parts
    for part in range(2):
        mine, other = last_product(
            place, early, late, early_part, pieces, sums, offsets, weights, width, part, after
        )
        after = mine[:1]
        other = swap(other, "col", 1)
        group = {
            q: add_low(mine[q], other[q * half : (q + 1) * half]) for q in range(chips)
        }
        groups.append(group)
    x_parts += [swap(part, "col", 1) for part in x_parts]
    cols = weights.shape[0]
    g = order_rows(place, pieces, sums, offsets, width, cols, groups[1][chips - 1])
    terms = [[group.pop(0)] for group in groups]
    whole = []
    bit = 1
    while bit < chips:
        for q in sorted((q for q in groups[0] if q & bit), reverse=True):
            sent = [group.pop(q) for group in groups]
            if q == bit and 2 * bit < chips:
                sent = jnp.concatenate(sent, axis=1)
                sent = lax.optimization_barrier((sent, received))[0]
                whole.append(swap(sent, "col", 2 * bit))
                continue
            arrived = [swap(half_sent, "col", 2 * bit) for half_sent in sent]
            received = arrived[0]
            for group, term, half in zip(groups, terms, arrived):
                if q == bit:
                    term.append(half)
                else:
                    group[q ^ bit] = add_low(group[q ^ bit], half)
        bit *= 2

    grad_wq, grad_wk, grad_wv = weight_grads(g, x_parts, order, w_query.shape[1])
    grad_input = sum_rows(terms, whole, grad_wk)
    return grad_input, grad_wq, grad_wk, grad_wv


def solution(mesh):
    return jax.shard_map(
        shards,
        mesh=mesh,
        in_specs=(
            P("col", "row"),
            P("row", "col"),
            P("row", "col"),
            P("row", "col"),
            P("row", "col"),
            P("row", "col"),
            P("row", "col"),
            P("row", "col"),
            P("row"),
            P("row"),
        ),
        out_specs=(P("col", "row"), P("row", "col"), P("row", "col"), P("row", "col")),
        check_vma=False,
    )
```

```python
import functools
import math

import jax
import jax.numpy as jnp
import numpy as np
from jax import lax
from jax.experimental import pallas as pl
from jax.experimental.pallas import tpu as pltpu
from jax.sharding import PartitionSpec as P

KEY_VALUE_HEADS = 8
HEAD_SIZE = 128
ROPE_BASE = 500000.0
PAD_ROWS = 16
MIB = 1024 * 1024


def contract(left, right, left_dim, right_dim):
    return lax.dot_general(
        left, right, (((left_dim,), (right_dim,)), ((), ())), preferred_element_type=jnp.float32
    )


def swap(value, axis, offset):
    pairs = [(source, source ^ offset) for source in range(lax.axis_size(axis))]
    return lax.ppermute(value, axis, pairs)


def gather_direct(value, axis):
    return [value] + [swap(value, axis, s) for s in range(1, lax.axis_size(axis))]


def add_low(left, right):
    return (left.astype(jnp.float32) + right.astype(jnp.float32)).astype(jnp.bfloat16)


def block_index(position, row, blocks, tokens):
    index = position
    for b in range(blocks):
        index = jnp.where(position >= b * tokens, position + ((row ^ b) - b) * tokens, index)
    return index.astype(jnp.float32)


def unrotate(gradient, cosine, sine):
    return gradient * cosine + pltpu.roll(gradient, HEAD_SIZE // 2, 1) * sine


def pack_kernel(k_ref, v_ref, ids_ref, out_ref):
    tokens = k_ref.shape[0]
    out_ref[:tokens, :HEAD_SIZE] = k_ref[...]
    out_ref[:tokens, HEAD_SIZE:] = v_ref[...]
    width = ids_ref.shape[1]
    row = lax.broadcasted_iota(jnp.int32, (PAD_ROWS, width), 0)
    ids = jnp.ones((PAD_ROWS, width), jnp.float32)
    for i in range(ids_ref.shape[0]):
        ids = jnp.where(row == i, ids_ref[i : i + 1, :].astype(jnp.float32), ids)
    out_ref[tokens:, :] = jnp.ones((PAD_ROWS, out_ref.shape[1]), jnp.bfloat16)
    out_ref[tokens:, :width] = ids.astype(jnp.bfloat16)


def pack(key, value, segment_ids):
    tokens = key.shape[0]
    width = 2 * HEAD_SIZE
    rows = -(-tokens // width)
    ids = segment_ids
    if rows > 1:
        ids = jnp.pad(ids, (0, rows * width - tokens), constant_values=1)
    ids = ids.reshape(rows, -1)
    vmem = pl.BlockSpec(memory_space=pltpu.VMEM)
    return pl.pallas_call(
        pack_kernel,
        out_shape=jax.ShapeDtypeStruct((tokens + PAD_ROWS, width), jnp.bfloat16),
        in_specs=[vmem] * 3,
        out_specs=vmem,
        compiler_params=pltpu.CompilerParams(vmem_limit_bytes=MIB),
        cost_estimate=pl.CostEstimate(
            flops=0, bytes_accessed=8 * tokens * HEAD_SIZE, transcendentals=0
        ),
        name="pack",
    )(
        pltpu.with_memory_space_constraint(key, pltpu.HBM),
        pltpu.with_memory_space_constraint(value, pltpu.HBM),
        pltpu.with_memory_space_constraint(ids, pltpu.HBM),
    )


def prepare_kernel(heads, blocks, row_ref, q_hbm, o_hbm, positions_ref, ids_ref, freq_ref, *refs):
    q_ref, o_ref, cos_ref, sin_ref, sems = refs
    tokens = q_hbm.shape[0]
    row = row_ref[0]
    copies = []
    for h in range(heads):
        rows = slice(h * tokens, (h + 1) * tokens)
        cols = slice(h * HEAD_SIZE, (h + 1) * HEAD_SIZE)
        for i, (source, target) in enumerate(((q_hbm, q_ref), (o_hbm, o_ref))):
            copies.append(
                pltpu.make_async_copy(source.at[:, cols], target.at[rows, :], sems.at[h, i])
            )
            copies[-1].start()

    first = (row * tokens).astype(jnp.float32)
    last = first + (tokens - 1)
    positions = positions_ref[...].astype(jnp.float32)
    cut = first + jnp.sum(1.0 - ids_ref[...].astype(jnp.float32), axis=1, keepdims=True)
    offset_low = positions[:, :1] - first
    offset_high = positions[:, tokens - 1 :] - last
    place = lax.broadcasted_iota(jnp.int32, (blocks * tokens, 1), 0)
    index = block_index(place, row, blocks, tokens)
    angle = (index + jnp.where(index < cut, offset_low, offset_high)) * freq_ref[...]
    lane = lax.broadcasted_iota(jnp.int32, (1, HEAD_SIZE), 1)
    lower = lane < HEAD_SIZE // 2
    table = jnp.cos(angle - jnp.where(lower, 0.0, math.pi / 2))
    turned = pltpu.roll(table, HEAD_SIZE // 2, 1)
    cos_ref[...] = jnp.where(lower, table, turned)
    sin_ref[...] = jnp.where(lower, turned, -table)

    for copy in copies:
        copy.wait()


def prepare(row, blocks, query, out_grad, positions, segment_ids):
    tokens, width = query.shape
    heads = width // HEAD_SIZE
    half_width = HEAD_SIZE // 2
    freq = np.exp(-(2.0 * np.arange(half_width) / HEAD_SIZE) * math.log(ROPE_BASE))
    freq = np.tile(freq, 2)[None].astype(np.float32)
    vmem = pl.BlockSpec(memory_space=pltpu.VMEM)
    hbm = pl.BlockSpec(memory_space=pltpu.HBM)
    return pl.pallas_call(
        functools.partial(prepare_kernel, heads, blocks),
        out_shape=[jax.ShapeDtypeStruct((heads * tokens, HEAD_SIZE), jnp.bfloat16)] * 2
        + [jax.ShapeDtypeStruct((blocks * tokens, HEAD_SIZE), jnp.float32)] * 2,
        in_specs=[pl.BlockSpec(memory_space=pltpu.SMEM), hbm, hbm, vmem, vmem, vmem],
        out_specs=[vmem] * 4,
        scratch_shapes=[pltpu.SemaphoreType.DMA((heads, 2))],
        compiler_params=pltpu.CompilerParams(vmem_limit_bytes=8 * MIB),
        cost_estimate=pl.CostEstimate(
            flops=0,
            bytes_accessed=8 * tokens * width,
            transcendentals=2 * blocks * tokens * HEAD_SIZE,
        ),
        name="prepare",
    )(
        row,
        pltpu.with_memory_space_constraint(query, pltpu.HBM),
        pltpu.with_memory_space_constraint(out_grad, pltpu.HBM),
        pltpu.with_memory_space_constraint(positions.reshape(1, -1), pltpu.HBM),
        pltpu.with_memory_space_constraint(segment_ids.reshape(1, -1), pltpu.HBM),
        pltpu.with_memory_space_constraint(jnp.asarray(freq), pltpu.HBM),
    )


def attention_kernel(heads, blocks, row_ref, q_all, o_all, *refs):
    kv_refs = refs[:blocks]
    cos_ref, sin_ref = refs[blocks : blocks + 2]
    dq_refs, packet_refs = refs[blocks + 2 : blocks + 4], refs[blocks + 4 : blocks + 6]
    k_all, v_all, ds_all, w_all, bias_ref, scores_ref, dweights_ref = refs[blocks + 6 :]
    together = scores_ref.shape[0] // bias_ref.shape[0]
    tokens = q_all.shape[0] // heads
    width = dq_refs[0].shape[1]
    keys = tokens * blocks
    scale = HEAD_SIZE**-0.5
    row = row_ref[0]

    cut = jnp.zeros((1, 1), jnp.float32)
    for b in range(blocks):
        rows = slice(b * tokens, (b + 1) * tokens)
        k_all[rows, :] = kv_refs[b][:tokens, :HEAD_SIZE]
        v_all[rows, :] = kv_refs[b][:tokens, HEAD_SIZE:]
        first = 1.0 - kv_refs[b][tokens:, :].astype(jnp.float32)
        cut += jnp.sum(jnp.sum(first, axis=0, keepdims=True), axis=1, keepdims=True)
    lane = lax.broadcasted_iota(jnp.int32, (1, keys), 1)
    key_index = block_index(lane, row, blocks, tokens)
    query_index = (
        lax.broadcasted_iota(jnp.int32, (tokens, 1), 0) + row * tokens
    ).astype(jnp.float32)
    lowest = jnp.where(query_index < cut, 0.0, cut)
    visible = (key_index <= query_index) & (key_index >= lowest)
    bias_ref[...] = jnp.where(visible, 0.0, -1e30)

    for h in range(heads):
        if h % together == 0:
            rows = slice(h * tokens, (h + together) * tokens)
            scores_ref[...] = contract(q_all[rows, :], k_all[...], 1, 1)
            dweights_ref[...] = contract(o_all[rows, :], v_all[...], 1, 1)
        rows = slice(h % together * tokens, (h % together + 1) * tokens)
        scores = scores_ref[rows, :] + bias_ref[...]
        peak = jnp.max(scores, axis=1, keepdims=True)
        terms = jnp.exp2((scores - peak) * (scale * math.log2(math.e)))
        inverse = 1.0 / jnp.sum(terms, axis=1, keepdims=True)
        dweights = dweights_ref[rows, :]
        weights = terms * inverse
        delta = jnp.sum(weights * dweights, axis=1, keepdims=True)
        dscores = (weights * (dweights - delta) * scale).astype(jnp.bfloat16)
        rows = slice(h * tokens, (h + 1) * tokens)
        w_all[rows, :] = weights.astype(jnp.bfloat16)
        ds_all[rows, :] = dscores
    dq = contract(ds_all[...], k_all[...], 1, 0)
    for h in range(heads):
        side, first = divmod(h * HEAD_SIZE, width)
        cols = slice(first, first + HEAD_SIZE)
        head = dq[h * tokens : (h + 1) * tokens]
        head = unrotate(head, cos_ref[:tokens, :], sin_ref[:tokens, :]).astype(jnp.bfloat16)
        dq_refs[side][:, cols] = head
        packet_refs[side][:, cols] = head
    dk = contract(ds_all[...], q_all[...], 0, 0)
    dk = unrotate(dk, cos_ref[...], sin_ref[...]).astype(jnp.bfloat16)
    dv = contract(w_all[...], o_all[...], 0, 0).astype(jnp.bfloat16)
    for b in range(blocks):
        rows = slice(b * tokens, (b + 1) * tokens)
        cols = slice(width + b * HEAD_SIZE, width + (b + 1) * HEAD_SIZE)
        packet_refs[0][:, cols] = dk[rows]
        packet_refs[1][:, cols] = dv[rows]


def attention_backward(row, query, out_grad, packed, cosine, sine):
    blocks = len(packed)
    keys = cosine.shape[0]
    tokens = keys // blocks
    heads = query.shape[0] // tokens
    width = heads // 2 * HEAD_SIZE
    vmem = pl.BlockSpec(memory_space=pltpu.VMEM)
    return pl.pallas_call(
        functools.partial(attention_kernel, heads, blocks),
        out_shape=[jax.ShapeDtypeStruct((tokens, width), jnp.bfloat16)] * 2
        + [jax.ShapeDtypeStruct((tokens, width + blocks * HEAD_SIZE), jnp.bfloat16)] * 2,
        in_specs=[pl.BlockSpec(memory_space=pltpu.SMEM)] + [vmem] * (blocks + 4),
        out_specs=[vmem] * 4,
        scratch_shapes=[
            pltpu.VMEM((keys, HEAD_SIZE), jnp.bfloat16),
            pltpu.VMEM((keys, HEAD_SIZE), jnp.bfloat16),
            pltpu.VMEM((heads * tokens, keys), jnp.bfloat16),
            pltpu.VMEM((heads * tokens, keys), jnp.bfloat16),
            pltpu.VMEM((tokens, keys), jnp.float32),
            pltpu.VMEM((min(4, heads) * tokens, keys), jnp.float32),
            pltpu.VMEM((min(4, heads) * tokens, keys), jnp.float32),
        ],
        compiler_params=pltpu.CompilerParams(vmem_limit_bytes=32 * MIB),
        cost_estimate=pl.CostEstimate(
            flops=10 * heads * tokens * keys * HEAD_SIZE,
            bytes_accessed=16 * tokens * width + 16 * keys * HEAD_SIZE,
            transcendentals=heads * tokens * keys,
        ),
        name="attention_backward",
    )(row, query, out_grad, *packed, cosine, sine)


def combine_kernel(blocks, offset, columns, width, *refs):
    packet_ref, other_ref, out_ref = refs[0], refs[1], refs[-1]
    for i, first in enumerate(columns):
        out_ref[:, i * width : (i + 1) * width] = refs[2 + i][:, first : first + width]
    for b in range(blocks):
        first = len(columns) * width + b * HEAD_SIZE
        out_ref[:, first : first + HEAD_SIZE] = summed_block(
            packet_ref, other_ref, blocks, b, offset, slice(None)
        )


def summed_block(packet_ref, other_ref, blocks, b, offset, rows):
    def block_of(ref, index):
        first = ref.shape[1] - (blocks - index) * HEAD_SIZE
        if not isinstance(index, int):
            first = pl.multiple_of(first, HEAD_SIZE)
        return ref[rows, pl.ds(first, HEAD_SIZE)].astype(jnp.float32)

    total = block_of(packet_ref, b) + block_of(other_ref, b ^ offset)
    return total.astype(jnp.bfloat16)


def combine(packet, other, pieces, blocks, offset, width):
    tokens = packet.shape[0]
    cols = len(pieces) * width + blocks * HEAD_SIZE
    vmem = pl.BlockSpec(memory_space=pltpu.VMEM)
    return pl.pallas_call(
        functools.partial(combine_kernel, blocks, offset, [c for _, c in pieces], width),
        out_shape=jax.ShapeDtypeStruct((tokens, cols), jnp.bfloat16),
        in_specs=[vmem] * (2 + len(pieces)),
        out_specs=vmem,
        compiler_params=pltpu.CompilerParams(vmem_limit_bytes=4 * MIB),
        cost_estimate=pl.CostEstimate(
            flops=tokens * cols, bytes_accessed=6 * tokens * cols, transcendentals=0
        ),
        name="combine",
    )(packet, other, *[a for a, _ in pieces])


def spread(own, packet, bits, blocks):
    width = own.shape[1]
    held, newest, other, last = {0: (own, 0)}, {}, None, None
    for bit in bits:
        arrived = {}
        if newest:
            for offset, (array, first) in held.items():
                if array.shape[1] != width:
                    array = array[:, first : first + width]
                arrived[offset ^ bit] = (swap(array, "row", bit), 0)
            packet = combine(packet, other, list(newest.values()), blocks, last, width)
        sent = list(newest) if newest else [0]
        other = swap(packet, "row", bit)
        held.update(newest)
        arrived |= {offset ^ bit: (other, i * width) for i, offset in enumerate(sent)}
        newest, last = arrived, bit
    held.update(newest)
    return held, {offset ^ last for offset in sent}, packet, other, last


def turn_kernel(tile, wq_hbm, wk_hbm, wv_hbm, *refs):
    out_ref, wq, wk, wv, sems = refs[-5:]
    steps = wq.shape[0] // tile
    copies = []
    for j in range(steps):
        rows = slice(j * tile, (j + 1) * tile)
        copies.append(
            [
                pltpu.make_async_copy(source.at[rows, :], target.at[rows, :], sems.at[j, i])
                for i, (source, target) in enumerate(
                    ((wq_hbm, wq), (wk_hbm, wk), (wv_hbm, wv))
                )
            ]
        )
        for copy in copies[j]:
            copy.start()
    for j in range(steps):
        rows = slice(j * tile, (j + 1) * tile)
        first = 0
        for copy, weight in zip(copies[j], (wq, wk, wv)):
            copy.wait()
            out_ref[first : first + weight.shape[1], rows] = weight[rows, :].T
            first += weight.shape[1]


def turn_weights(weights, after):
    features = weights[0].shape[0]
    widths = [w.shape[1] for w in weights]
    tile = min(512, features)
    hbm = pl.BlockSpec(memory_space=pltpu.HBM)
    return pl.pallas_call(
        functools.partial(turn_kernel, tile),
        out_shape=pltpu.VMEM((sum(widths), features), jnp.bfloat16),
        in_specs=[hbm] * 3 + [pl.BlockSpec(memory_space=pl.ANY)] * len(after),
        out_specs=pl.BlockSpec(memory_space=pltpu.VMEM),
        scratch_shapes=[pltpu.VMEM((features, width), jnp.bfloat16) for width in widths]
        + [pltpu.SemaphoreType.DMA((features // tile, 3))],
        compiler_params=pltpu.CompilerParams(vmem_limit_bytes=16 * MIB),
        cost_estimate=pl.CostEstimate(
            flops=0, bytes_accessed=4 * features * sum(widths), transcendentals=0
        ),
        name="turn_weights",
    )(*[pltpu.with_memory_space_constraint(w, pltpu.HBM) for w in weights], *after)


def early_kernel(columns, tile, *refs):
    count, width = len(columns[0]), refs[-1].shape[1] // 2
    w_ref, out_ref, gq = refs[2 * count :]
    tokens = refs[0].shape[0]
    for i in range(2):
        for k, first in enumerate(columns[i]):
            gq[k * tokens : (k + 1) * tokens, i * width : (i + 1) * width] = refs[
                i * count + k
            ][:, first : first + width]
    for j in range(w_ref.shape[1] // tile):
        cols = slice(j * tile, (j + 1) * tile)
        out_ref[:, cols] = contract(gq[...], w_ref[: 2 * width, cols], 1, 0).astype(
            jnp.bfloat16
        )


def early_product(pieces, blocks, width, weights):
    arrays = [side[b][0] for side in pieces for b in blocks]
    columns = [[side[b][1] for b in blocks] for side in pieces]
    tokens = arrays[0].shape[0]
    features = weights.shape[1]
    tile = min(1024, features)
    rows = len(blocks) * tokens
    vmem = pl.BlockSpec(memory_space=pltpu.VMEM)
    return pl.pallas_call(
        functools.partial(early_kernel, columns, tile),
        out_shape=jax.ShapeDtypeStruct((rows, features), jnp.bfloat16),
        in_specs=[vmem] * (len(arrays) + 1),
        out_specs=vmem,
        scratch_shapes=[pltpu.VMEM((rows, 2 * width), jnp.bfloat16)],
        compiler_params=pltpu.CompilerParams(vmem_limit_bytes=16 * MIB),
        cost_estimate=pl.CostEstimate(
            flops=4 * rows * features * width,
            bytes_accessed=4 * features * width + 2 * rows * features + 4 * rows * width,
            transcendentals=0,
        ),
        name="early_product",
    )(*arrays, weights)


def put_pair(target_ref, target, first, sums, offsets, blocks, b, start):
    count = target.stop - target.start
    if offsets is None:
        tokens = sums[0].shape[0] // blocks
        rows = pl.ds(pl.multiple_of(b * tokens + start, 16), count)
        target_ref[target, first:] = sums[0][rows, :]
        return
    rows = pl.ds(pl.multiple_of(start, 16), count)
    for i in range(2):
        cols = slice(first + i * HEAD_SIZE, first + (i + 1) * HEAD_SIZE)
        target_ref[target, cols] = summed_block(
            sums[2 * i], sums[2 * i + 1], blocks, b, offsets[i], rows
        )


def by_destination(blocks, half, place_ref, put):
    core, turn = place_ref[0], place_ref[1]
    for q in range(blocks):
        for b in range(blocks):

            @pl.when((q ^ turn) == b)
            def _():
                for side in range(2):
                    first = (side * blocks + q) * half
                    put(q, side, slice(first, first + half), b, (core ^ side) * half)


def place_in(members, b):
    place, found = jnp.int32(0), jnp.bool_(False)
    for i, member in enumerate(members):
        place = jnp.where(b == member, i, place)
        found = found | (b == member)
    return place, found


def last_kernel(early, late, columns, offsets, part, width, spare, place_ref, *refs):
    blocks = len(early) + len(late)
    early_ref, w_ref, refs = refs[0], refs[1], refs[2 + spare :]
    pieces = [refs[i * len(late) : (i + 1) * len(late)] for i in range(2)]
    refs = refs[2 * len(late) :]
    count = 1 if offsets is None else 4
    sums, refs = refs[:count], refs[count:]
    mine_refs, other_ref, gq, gkv, query, pair = refs[:blocks], *refs[blocks:]
    half = mine_refs[0].shape[0]
    tokens = 2 * half
    cols = slice(part * other_ref.shape[1], (part + 1) * other_ref.shape[1])

    for i in range(2):
        for k, first in enumerate(columns[i]):
            gq[k * tokens : (k + 1) * tokens, i * width : (i + 1) * width] = pieces[i][k][
                :, first : first + width
            ]

    core, turn = place_ref[0], place_ref[1]
    targets = [
        (q, side, slice((side * blocks + q) * half, (side * blocks + q + 1) * half))
        for q in range(blocks)
        for side in range(2)
    ]
    for q, side, target in targets:
        put_pair(gkv, target, 0, sums, offsets, blocks, q ^ turn, (core ^ side) * half)
    query[...] = contract(gq[...], w_ref[: 2 * width, cols], 1, 0).astype(jnp.bfloat16)
    pair[...] = contract(gkv[...], w_ref[2 * width :, cols], 1, 0)

    for q, side, target in targets:
        early_place, in_early = place_in(early, q ^ turn)
        late_place, in_late = place_in(late, q ^ turn)
        out_ref = other_ref.at[q * half : (q + 1) * half, :] if side else mine_refs[q]

        def put(part_ref, place, part_cols):
            start = place * tokens + (core ^ side) * half
            rows = pl.ds(pl.multiple_of(start, 16), half)
            total = pair[target, :] + part_ref[rows, part_cols].astype(jnp.float32)
            out_ref[...] = total.astype(jnp.bfloat16)

        pl.when(in_early)(functools.partial(put, early_ref, early_place, cols))
        pl.when(in_late)(functools.partial(put, query, late_place, slice(None)))


def last_product(place, early, late, early_part, pieces, sums, offsets, weights, width, part, after):
    blocks = len(early) + len(late)
    arrays = [side[b][0] for side in pieces for b in late]
    columns = [[side[b][1] for b in late] for side in pieces]
    tokens = arrays[0].shape[0]
    half, cols = tokens // 2, weights.shape[1] // 2
    pair_cols = weights.shape[0] - 2 * width
    vmem = pl.BlockSpec(memory_space=pltpu.VMEM)
    *mine, other = pl.pallas_call(
        functools.partial(
            last_kernel, early, late, columns, offsets, part, width, len(after)
        ),
        out_shape=[jax.ShapeDtypeStruct((half, cols), jnp.bfloat16)] * blocks
        + [jax.ShapeDtypeStruct((blocks * half, cols), jnp.bfloat16)],
        in_specs=[pl.BlockSpec(memory_space=pltpu.SMEM)]
        + [vmem] * 2
        + [pl.BlockSpec(memory_space=pl.ANY)] * len(after)
        + [vmem] * (len(arrays) + len(sums)),
        out_specs=[vmem] * (blocks + 1),
        scratch_shapes=[
            pltpu.VMEM((len(late) * tokens, 2 * width), jnp.bfloat16),
            pltpu.VMEM((blocks * tokens, pair_cols), jnp.bfloat16),
            pltpu.VMEM((len(late) * tokens, cols), jnp.bfloat16),
            pltpu.VMEM((blocks * tokens, cols), jnp.float32),
        ],
        compiler_params=pltpu.CompilerParams(vmem_limit_bytes=16 * MIB),
        cost_estimate=pl.CostEstimate(
            flops=2 * tokens * cols * (len(late) * 2 * width + blocks * pair_cols),
            bytes_accessed=2 * cols * (2 * width + pair_cols) + 8 * blocks * tokens * cols,
            transcendentals=0,
        ),
        name="last_product",
    )(place, early_part, weights, *after, *arrays, *sums)
    return mine, other


def order_kernel(blocks, columns, offsets, width, place_ref, *refs):
    pieces = [refs[i * blocks : (i + 1) * blocks] for i in range(2)]
    sums, g = refs[2 * blocks : -2], refs[-1]
    half = g.shape[0] // (2 * blocks)

    def put(q, side, target, b, start):
        rows = pl.ds(pl.multiple_of(start, 16), half)
        for i in range(2):
            first = columns[i][b]
            g[target, i * width : (i + 1) * width] = pieces[i][b][rows, first : first + width]
        put_pair(g, target, 2 * width, sums, offsets, blocks, b, start)

    by_destination(blocks, half, place_ref, put)


def order_rows(place, pieces, sums, offsets, width, cols, after):
    blocks = len(pieces[0])
    arrays = [side[b][0] for side in pieces for b in range(blocks)]
    columns = [[side[b][1] for b in range(blocks)] for side in pieces]
    rows = blocks * arrays[0].shape[0]
    vmem = pl.BlockSpec(memory_space=pltpu.VMEM)
    return pl.pallas_call(
        functools.partial(order_kernel, blocks, columns, offsets, width),
        out_shape=jax.ShapeDtypeStruct((rows, cols), jnp.bfloat16),
        in_specs=[pl.BlockSpec(memory_space=pltpu.SMEM)]
        + [vmem] * (len(arrays) + len(sums))
        + [pl.BlockSpec(memory_space=pl.ANY)],
        out_specs=vmem,
        compiler_params=pltpu.CompilerParams(vmem_limit_bytes=8 * MIB),
        cost_estimate=pl.CostEstimate(
            flops=0, bytes_accessed=4 * rows * cols, transcendentals=0
        ),
        name="order_rows",
    )(place, *arrays, *sums, after)


def join_kernel(count, *refs):
    sources, out_ref, sems = refs[:count], refs[count + 1], refs[count + 2]
    rows = sources[0].shape[0]
    copies = [
        pltpu.make_async_copy(source, out_ref.at[i * rows : (i + 1) * rows, :], sems.at[i])
        for i, source in enumerate(sources)
    ]
    for copy in copies:
        copy.start()
    for copy in copies:
        copy.wait()


def join_rows(arrays, after):
    count = len(arrays)
    rows, cols = arrays[0].shape
    return pl.pallas_call(
        functools.partial(join_kernel, count),
        out_shape=jax.ShapeDtypeStruct((count * rows, cols), arrays[0].dtype),
        in_specs=[pl.BlockSpec(memory_space=pl.ANY)] * (count + 1),
        out_specs=pl.BlockSpec(memory_space=pltpu.VMEM),
        scratch_shapes=[pltpu.SemaphoreType.DMA((count,))],
        compiler_params=pltpu.CompilerParams(vmem_limit_bytes=4 * MIB),
        cost_estimate=pl.CostEstimate(
            flops=0, bytes_accessed=4 * count * rows * cols, transcendentals=0
        ),
        name="join_rows",
    )(*arrays, after)


def weight_grad_kernel(places, g_ref, *refs):
    pieces = len(places)
    x_refs = refs[:pieces]
    gwq_ref, gwk_ref, gwv_ref, x_all = refs[pieces:]
    query_cols, key_cols = gwq_ref.shape[1], gwk_ref.shape[1]
    rows = x_refs[0].shape[0]
    for place, x_ref in zip(places, x_refs):
        x_all[place * rows : (place + 1) * rows, :] = x_ref[...]
    x = x_all[...]
    gwq_ref[...] = contract(x, g_ref[:, :query_cols], 0, 0)
    pair = contract(x, g_ref[:, query_cols:], 0, 0)
    gwk_ref[...] = pair[:, :key_cols]
    gwv_ref[...] = pair[:, key_cols:]


def weight_grads(g, x_parts, order, query_cols):
    chips = len(order)
    features = x_parts[0].shape[1]
    piece_tokens = g.shape[0] // (2 * chips)
    places = [core * chips + q for core in range(2) for q in order]
    counts = [part.shape[0] // piece_tokens for part in x_parts]
    key_cols = (g.shape[1] - query_cols) // 2
    tile = min(256, features)
    return pl.pallas_call(
        functools.partial(weight_grad_kernel, places),
        grid=(features // tile,),
        out_shape=[
            jax.ShapeDtypeStruct((features, query_cols), jnp.float32),
            jax.ShapeDtypeStruct((features, key_cols), jnp.float32),
            jax.ShapeDtypeStruct((features, key_cols), jnp.float32),
        ],
        in_specs=[pl.BlockSpec(g.shape, lambda i: (0, 0))]
        + [
            pl.BlockSpec((piece_tokens, tile), lambda i, k=k: (k, i))
            for count in counts
            for k in range(count)
        ],
        out_specs=[
            pl.BlockSpec((tile, query_cols), lambda i: (i, 0)),
            pl.BlockSpec((tile, key_cols), lambda i: (i, 0)),
            pl.BlockSpec((tile, key_cols), lambda i: (i, 0)),
        ],
        scratch_shapes=[pltpu.VMEM((g.shape[0], tile), jnp.bfloat16)],
        compiler_params=pltpu.CompilerParams(vmem_limit_bytes=32 * MIB),
        cost_estimate=pl.CostEstimate(
            flops=2 * g.size * features,
            bytes_accessed=2 * g.size + 2 * g.shape[0] * features + 4 * features * g.shape[1],
            transcendentals=0,
        ),
        name="weight_grads",
    )(g, *[x for x, n in zip(x_parts, counts) for _ in range(n)])


def sum_kernel(count, groups, *refs):
    out_ref = refs[-1]
    for i in range(groups):
        cols = slice(
            i * out_ref.shape[1] // groups, (i + 1) * out_ref.shape[1] // groups
        )
        total = refs[i * count][...].astype(jnp.float32)
        for ref in refs[i * count + 1 : (i + 1) * count]:
            total += ref[...].astype(jnp.float32)
        for ref in refs[groups * count : -2]:
            total += ref[:, cols].astype(jnp.float32)
        out_ref[:, cols] = total.astype(out_ref.dtype)


def sum_rows(groups, whole, after):
    rows, cols = groups[0][0].shape
    terms = [term for group in groups for term in group] + whole
    vmem = pl.BlockSpec(memory_space=pltpu.VMEM)
    return pl.pallas_call(
        functools.partial(sum_kernel, len(groups[0]), len(groups)),
        out_shape=jax.ShapeDtypeStruct((rows, cols * len(groups)), jnp.bfloat16),
        in_specs=[vmem] * len(terms) + [pl.BlockSpec(memory_space=pl.ANY)],
        out_specs=vmem,
        compiler_params=pltpu.CompilerParams(vmem_limit_bytes=4 * MIB),
        cost_estimate=pl.CostEstimate(
            flops=len(terms) * rows * cols,
            bytes_accessed=4 * len(terms) * rows * cols,
            transcendentals=0,
        ),
        name="sum_rows",
    )(*terms, pltpu.with_memory_space_constraint(after, pltpu.HBM))


def shards(
    layer_input,
    w_query,
    w_key,
    w_value,
    rotated_query_state,
    rotated_key_state,
    saved_value_state,
    context_gradient,
    positions,
    segment_ids,
):
    tokens = rotated_query_state.shape[0]
    n_row, n_col = lax.axis_size("row"), lax.axis_size("col")
    chips = n_col // 2
    shared_heads = n_col // KEY_VALUE_HEADS
    row_index = lax.axis_index("row").astype(jnp.int32)
    col_index = lax.axis_index("col").astype(jnp.int32)
    chip_index, core_index = col_index // 2, col_index % 2

    key, value = rotated_key_state, saved_value_state
    if shared_heads > 1:
        pair = jnp.concatenate([key, value], axis=1)
        pair = [pair] + [swap(pair, "col", s) for s in range(1, shared_heads)]
        part = col_index % shared_heads
        stacked = jnp.stack(pair)
        stacked = jnp.take(stacked, jnp.arange(shared_heads) ^ part, axis=0)
        stacked = stacked.reshape(shared_heads, tokens, 2, -1).transpose(1, 2, 0, 3)
        stacked = stacked.reshape(tokens, 2, HEAD_SIZE)
        key, value = stacked[:, 0], stacked[:, 1]
    packed = gather_direct(pack(key, value, segment_ids), "row")

    row = row_index.reshape(1)
    query, out_grad, cosine, sine = prepare(
        row, n_row, rotated_query_state, context_gradient, positions, segment_ids
    )
    first, second, *packets = attention_backward(row, query, out_grad, packed, cosine, sine)
    bits = [1 << i for i in range(n_row.bit_length() - 1)]
    pieces, sums, offsets, late = [], [], [], set()
    for own, packet, order in zip((first, second), packets, (bits, bits[::-1])):
        held, with_last, *last_two, offset = spread(own, packet, order, n_row)
        pieces.append(held)
        late |= with_last
        sums += last_two
        offsets.append(offset)

    if shared_heads > 1:
        dkv = []
        for i in range(2):
            packet, other = (a[:, -n_row * HEAD_SIZE :] for a in sums[2 * i : 2 * i + 2])
            packet, other = (a.reshape(tokens, n_row, HEAD_SIZE) for a in (packet, other))
            dkv.append(add_low(packet, other[:, np.arange(n_row) ^ offsets[i]]))
        dkv = jnp.stack(dkv, axis=2)
        bit = shared_heads // 2
        while bit:
            half = dkv.shape[3] // 2
            upper = (col_index & bit) != 0
            lower_part, upper_part = dkv[..., :half], dkv[..., half:]
            kept = jnp.where(upper, upper_part, lower_part)
            sent = jnp.where(upper, lower_part, upper_part)
            dkv = add_low(kept, swap(sent, "col", bit))
            bit //= 2
        sums, offsets = [dkv.transpose(1, 0, 2, 3).reshape(n_row * tokens, -1)], None

    held, order = layer_input, [0]
    bit = chips // 2
    while bit > 1:
        held = join_rows([held, swap(held, "col", 2 * bit)], first)
        order += [q | bit for q in order]
        bit //= 2
    x_parts = [held, swap(held, "col", 2)]
    order += [q | 1 for q in order]

    place = jnp.stack([core_index, row_index ^ chip_index])
    weights = turn_weights((w_query, w_key, w_value), [sums[0]])
    weights = pltpu.with_memory_space_constraint(weights, pltpu.VMEM)
    width = first.shape[1]
    early = [b for b in range(n_row) if b not in late]
    late = sorted(late)
    early_part = early_product(pieces, early, width, weights)
    half = tokens // 2
    groups, after = [], x_parts
    for part in range(2):
        mine, other = last_product(
            place, early, late, early_part, pieces, sums, offsets, weights, width, part, after
        )
        after = mine[:1]
        other = swap(other, "col", 1)
        group = {
            q: add_low(mine[q], other[q * half : (q + 1) * half]) for q in range(chips)
        }
        groups.append(group)
    x_parts += [swap(part, "col", 1) for part in x_parts]
    cols = weights.shape[0]
    g = order_rows(place, pieces, sums, offsets, width, cols, groups[1][chips - 1])
    terms = [[group.pop(0)] for group in groups]
    whole = []
    bit = 1
    while bit < chips:
        for q in sorted((q for q in groups[0] if q & bit), reverse=True):
            sent = [group.pop(q) for group in groups]
            if q == bit and 2 * bit < chips:
                sent = jnp.concatenate(sent, axis=1)
                sent = lax.optimization_barrier((sent, received))[0]
                whole.append(swap(sent, "col", 2 * bit))
                continue
            for group, term, half_sent in zip(groups, terms, sent):
                received = swap(half_sent, "col", 2 * bit)
                if q == bit:
                    term.append(received)
                else:
                    group[q ^ bit] = add_low(group[q ^ bit], received)
        bit *= 2

    grad_wq, grad_wk, grad_wv = weight_grads(g, x_parts, order, w_query.shape[1])
    grad_input = sum_rows(terms, whole, grad_wk)
    return grad_input, grad_wq, grad_wk, grad_wv


def solution(mesh):
    return jax.shard_map(
        shards,
        mesh=mesh,
        in_specs=(
            P("col", "row"),
            P("row", "col"),
            P("row", "col"),
            P("row", "col"),
            P("row", "col"),
            P("row", "col"),
            P("row", "col"),
            P("row", "col"),
            P("row"),
            P("row"),
        ),
        out_specs=(P("col", "row"), P("row", "col"), P("row", "col"), P("row", "col")),
        check_vma=False,
    )
```

```python
import functools
import math

import jax
import jax.numpy as jnp
import numpy as np
from jax import lax
from jax.experimental import pallas as pl
from jax.experimental.pallas import tpu as pltpu
from jax.sharding import PartitionSpec as P

KEY_VALUE_HEADS = 8
HEAD_SIZE = 128
ROPE_BASE = 500000.0
PAD_ROWS = 16
MIB = 1024 * 1024


def contract(left, right, left_dim, right_dim):
    return lax.dot_general(
        left, right, (((left_dim,), (right_dim,)), ((), ())), preferred_element_type=jnp.float32
    )


def swap(value, axis, offset):
    pairs = [(source, source ^ offset) for source in range(lax.axis_size(axis))]
    return lax.ppermute(value, axis, pairs)


def gather_direct(value, axis):
    return [value] + [swap(value, axis, s) for s in range(1, lax.axis_size(axis))]


def add_low(left, right):
    return (left.astype(jnp.float32) + right.astype(jnp.float32)).astype(jnp.bfloat16)


def block_index(position, row, blocks, tokens):
    index = position
    for b in range(blocks):
        index = jnp.where(position >= b * tokens, position + ((row ^ b) - b) * tokens, index)
    return index.astype(jnp.float32)


def unrotate(gradient, cosine, sine):
    return gradient * cosine + pltpu.roll(gradient, HEAD_SIZE // 2, 1) * sine


def pack_kernel(k_ref, v_ref, ids_ref, out_ref):
    tokens = k_ref.shape[0]
    out_ref[:tokens, :HEAD_SIZE] = k_ref[...]
    out_ref[:tokens, HEAD_SIZE:] = v_ref[...]
    width = ids_ref.shape[1]
    row = lax.broadcasted_iota(jnp.int32, (PAD_ROWS, width), 0)
    ids = jnp.ones((PAD_ROWS, width), jnp.float32)
    for i in range(ids_ref.shape[0]):
        ids = jnp.where(row == i, ids_ref[i : i + 1, :].astype(jnp.float32), ids)
    out_ref[tokens:, :] = jnp.ones((PAD_ROWS, out_ref.shape[1]), jnp.bfloat16)
    out_ref[tokens:, :width] = ids.astype(jnp.bfloat16)


def pack(key, value, segment_ids):
    tokens = key.shape[0]
    width = 2 * HEAD_SIZE
    rows = -(-tokens // width)
    ids = segment_ids
    if rows > 1:
        ids = jnp.pad(ids, (0, rows * width - tokens), constant_values=1)
    ids = ids.reshape(rows, -1)
    vmem = pl.BlockSpec(memory_space=pltpu.VMEM)
    return pl.pallas_call(
        pack_kernel,
        out_shape=jax.ShapeDtypeStruct((tokens + PAD_ROWS, width), jnp.bfloat16),
        in_specs=[vmem] * 3,
        out_specs=vmem,
        compiler_params=pltpu.CompilerParams(vmem_limit_bytes=MIB),
        cost_estimate=pl.CostEstimate(
            flops=0, bytes_accessed=8 * tokens * HEAD_SIZE, transcendentals=0
        ),
        name="pack",
    )(
        pltpu.with_memory_space_constraint(key, pltpu.HBM),
        pltpu.with_memory_space_constraint(value, pltpu.HBM),
        pltpu.with_memory_space_constraint(ids, pltpu.HBM),
    )


def prepare_kernel(heads, blocks, row_ref, q_hbm, o_hbm, positions_ref, ids_ref, freq_ref, *refs):
    q_ref, o_ref, cos_ref, sin_ref, sems = refs
    tokens = q_hbm.shape[0]
    row = row_ref[0]
    copies = []
    for h in range(heads):
        rows = slice(h * tokens, (h + 1) * tokens)
        cols = slice(h * HEAD_SIZE, (h + 1) * HEAD_SIZE)
        for i, (source, target) in enumerate(((q_hbm, q_ref), (o_hbm, o_ref))):
            copies.append(
                pltpu.make_async_copy(source.at[:, cols], target.at[rows, :], sems.at[h, i])
            )
            copies[-1].start()

    first = (row * tokens).astype(jnp.float32)
    last = first + (tokens - 1)
    positions = positions_ref[...].astype(jnp.float32)
    cut = first + jnp.sum(1.0 - ids_ref[...].astype(jnp.float32), axis=1, keepdims=True)
    offset_low = positions[:, :1] - first
    offset_high = positions[:, tokens - 1 :] - last
    place = lax.broadcasted_iota(jnp.int32, (blocks * tokens, 1), 0)
    index = block_index(place, row, blocks, tokens)
    angle = (index + jnp.where(index < cut, offset_low, offset_high)) * freq_ref[...]
    lane = lax.broadcasted_iota(jnp.int32, (1, HEAD_SIZE), 1)
    lower = lane < HEAD_SIZE // 2
    table = jnp.cos(angle - jnp.where(lower, 0.0, math.pi / 2))
    turned = pltpu.roll(table, HEAD_SIZE // 2, 1)
    cos_ref[...] = jnp.where(lower, table, turned)
    sin_ref[...] = jnp.where(lower, turned, -table)

    for copy in copies:
        copy.wait()


def prepare(row, blocks, query, out_grad, positions, segment_ids):
    tokens, width = query.shape
    heads = width // HEAD_SIZE
    half_width = HEAD_SIZE // 2
    freq = np.exp(-(2.0 * np.arange(half_width) / HEAD_SIZE) * math.log(ROPE_BASE))
    freq = np.tile(freq, 2)[None].astype(np.float32)
    vmem = pl.BlockSpec(memory_space=pltpu.VMEM)
    hbm = pl.BlockSpec(memory_space=pltpu.HBM)
    return pl.pallas_call(
        functools.partial(prepare_kernel, heads, blocks),
        out_shape=[jax.ShapeDtypeStruct((heads * tokens, HEAD_SIZE), jnp.bfloat16)] * 2
        + [jax.ShapeDtypeStruct((blocks * tokens, HEAD_SIZE), jnp.float32)] * 2,
        in_specs=[pl.BlockSpec(memory_space=pltpu.SMEM), hbm, hbm, vmem, vmem, vmem],
        out_specs=[vmem] * 4,
        scratch_shapes=[pltpu.SemaphoreType.DMA((heads, 2))],
        compiler_params=pltpu.CompilerParams(vmem_limit_bytes=8 * MIB),
        cost_estimate=pl.CostEstimate(
            flops=0,
            bytes_accessed=8 * tokens * width,
            transcendentals=2 * blocks * tokens * HEAD_SIZE,
        ),
        name="prepare",
    )(
        row,
        pltpu.with_memory_space_constraint(query, pltpu.HBM),
        pltpu.with_memory_space_constraint(out_grad, pltpu.HBM),
        pltpu.with_memory_space_constraint(positions.reshape(1, -1), pltpu.HBM),
        pltpu.with_memory_space_constraint(segment_ids.reshape(1, -1), pltpu.HBM),
        pltpu.with_memory_space_constraint(jnp.asarray(freq), pltpu.HBM),
    )


def attention_kernel(heads, blocks, row_ref, q_all, o_all, *refs):
    kv_refs = refs[:blocks]
    cos_ref, sin_ref = refs[blocks : blocks + 2]
    dq_refs, packet_refs = refs[blocks + 2 : blocks + 4], refs[blocks + 4 : blocks + 6]
    k_all, v_all, ds_all, w_all, bias_ref, scores_ref, dweights_ref = refs[blocks + 6 :]
    together = min(4, heads)
    tokens = q_all.shape[0] // heads
    width = dq_refs[0].shape[1]
    keys = tokens * blocks
    scale = HEAD_SIZE**-0.5
    row = row_ref[0]

    cut = jnp.zeros((1, 1), jnp.float32)
    for b in range(blocks):
        rows = slice(b * tokens, (b + 1) * tokens)
        k_all[rows, :] = kv_refs[b][:tokens, :HEAD_SIZE]
        v_all[rows, :] = kv_refs[b][:tokens, HEAD_SIZE:]
        first = 1.0 - kv_refs[b][tokens:, :].astype(jnp.float32)
        cut += jnp.sum(jnp.sum(first, axis=0, keepdims=True), axis=1, keepdims=True)
    lane = lax.broadcasted_iota(jnp.int32, (1, keys), 1)
    key_index = block_index(lane, row, blocks, tokens)
    query_index = (
        lax.broadcasted_iota(jnp.int32, (tokens, 1), 0) + row * tokens
    ).astype(jnp.float32)
    lowest = jnp.where(query_index < cut, 0.0, cut)
    visible = (key_index <= query_index) & (key_index >= lowest)
    bias_ref[...] = jnp.where(visible, 0.0, -1e30)

    for h in range(heads):
        if h % together == 0:
            rows = slice(h * tokens, (h + together) * tokens)
            scores_ref[rows, :] = contract(q_all[rows, :], k_all[...], 1, 1)
            dweights_ref[rows, :] = contract(o_all[rows, :], v_all[...], 1, 1)
        rows = slice(h * tokens, (h + 1) * tokens)
        scores = scores_ref[rows, :] + bias_ref[...]
        peak = jnp.max(scores, axis=1, keepdims=True)
        terms = jnp.exp2((scores - peak) * (scale * math.log2(math.e)))
        inverse = 1.0 / jnp.sum(terms, axis=1, keepdims=True)
        dweights = dweights_ref[rows, :]
        weights = terms * inverse
        delta = jnp.sum(weights * dweights, axis=1, keepdims=True)
        dscores = (weights * (dweights - delta) * scale).astype(jnp.bfloat16)
        w_all[rows, :] = weights.astype(jnp.bfloat16)
        ds_all[rows, :] = dscores
    dq = contract(ds_all[...], k_all[...], 1, 0)
    for h in range(heads):
        side, first = divmod(h * HEAD_SIZE, width)
        cols = slice(first, first + HEAD_SIZE)
        head = dq[h * tokens : (h + 1) * tokens]
        head = unrotate(head, cos_ref[:tokens, :], sin_ref[:tokens, :]).astype(jnp.bfloat16)
        dq_refs[side][:, cols] = head
        packet_refs[side][:, cols] = head
    dk = contract(ds_all[...], q_all[...], 0, 0)
    dk = unrotate(dk, cos_ref[...], sin_ref[...]).astype(jnp.bfloat16)
    dv = contract(w_all[...], o_all[...], 0, 0).astype(jnp.bfloat16)
    for b in range(blocks):
        rows = slice(b * tokens, (b + 1) * tokens)
        cols = slice(width + b * HEAD_SIZE, width + (b + 1) * HEAD_SIZE)
        packet_refs[0][:, cols] = dk[rows]
        packet_refs[1][:, cols] = dv[rows]


def attention_backward(row, query, out_grad, packed, cosine, sine):
    blocks = len(packed)
    keys = cosine.shape[0]
    tokens = keys // blocks
    heads = query.shape[0] // tokens
    width = heads // 2 * HEAD_SIZE
    vmem = pl.BlockSpec(memory_space=pltpu.VMEM)
    return pl.pallas_call(
        functools.partial(attention_kernel, heads, blocks),
        out_shape=[jax.ShapeDtypeStruct((tokens, width), jnp.bfloat16)] * 2
        + [jax.ShapeDtypeStruct((tokens, width + blocks * HEAD_SIZE), jnp.bfloat16)] * 2,
        in_specs=[pl.BlockSpec(memory_space=pltpu.SMEM)] + [vmem] * (blocks + 4),
        out_specs=[vmem] * 4,
        scratch_shapes=[
            pltpu.VMEM((keys, HEAD_SIZE), jnp.bfloat16),
            pltpu.VMEM((keys, HEAD_SIZE), jnp.bfloat16),
            pltpu.VMEM((heads * tokens, keys), jnp.bfloat16),
            pltpu.VMEM((heads * tokens, keys), jnp.bfloat16),
            pltpu.VMEM((tokens, keys), jnp.float32),
            pltpu.VMEM((heads * tokens, keys), jnp.float32),
            pltpu.VMEM((heads * tokens, keys), jnp.float32),
        ],
        compiler_params=pltpu.CompilerParams(vmem_limit_bytes=32 * MIB),
        cost_estimate=pl.CostEstimate(
            flops=10 * heads * tokens * keys * HEAD_SIZE,
            bytes_accessed=16 * tokens * width + 16 * keys * HEAD_SIZE,
            transcendentals=heads * tokens * keys,
        ),
        name="attention_backward",
    )(row, query, out_grad, *packed, cosine, sine)


def combine_kernel(blocks, offset, columns, width, *refs):
    packet_ref, other_ref, out_ref = refs[0], refs[1], refs[-1]
    for i, first in enumerate(columns):
        out_ref[:, i * width : (i + 1) * width] = refs[2 + i][:, first : first + width]
    for b in range(blocks):
        first = len(columns) * width + b * HEAD_SIZE
        out_ref[:, first : first + HEAD_SIZE] = summed_block(
            packet_ref, other_ref, blocks, b, offset, slice(None)
        )


def summed_block(packet_ref, other_ref, blocks, b, offset, rows):
    def block_of(ref, index):
        first = ref.shape[1] - (blocks - index) * HEAD_SIZE
        if not isinstance(index, int):
            first = pl.multiple_of(first, HEAD_SIZE)
        return ref[rows, pl.ds(first, HEAD_SIZE)].astype(jnp.float32)

    total = block_of(packet_ref, b) + block_of(other_ref, b ^ offset)
    return total.astype(jnp.bfloat16)


def combine(packet, other, pieces, blocks, offset, width):
    tokens = packet.shape[0]
    cols = len(pieces) * width + blocks * HEAD_SIZE
    vmem = pl.BlockSpec(memory_space=pltpu.VMEM)
    return pl.pallas_call(
        functools.partial(combine_kernel, blocks, offset, [c for _, c in pieces], width),
        out_shape=jax.ShapeDtypeStruct((tokens, cols), jnp.bfloat16),
        in_specs=[vmem] * (2 + len(pieces)),
        out_specs=vmem,
        compiler_params=pltpu.CompilerParams(vmem_limit_bytes=4 * MIB),
        cost_estimate=pl.CostEstimate(
            flops=tokens * cols, bytes_accessed=6 * tokens * cols, transcendentals=0
        ),
        name="combine",
    )(packet, other, *[a for a, _ in pieces])


def spread(own, packet, bits, blocks):
    width = own.shape[1]
    held, newest, other, last = {0: (own, 0)}, {}, None, None
    for bit in bits:
        arrived = {}
        if newest:
            for offset, (array, first) in held.items():
                if array.shape[1] != width:
                    array = array[:, first : first + width]
                arrived[offset ^ bit] = (swap(array, "row", bit), 0)
            packet = combine(packet, other, list(newest.values()), blocks, last, width)
        sent = list(newest) if newest else [0]
        other = swap(packet, "row", bit)
        held.update(newest)
        arrived |= {offset ^ bit: (other, i * width) for i, offset in enumerate(sent)}
        newest, last = arrived, bit
    held.update(newest)
    return held, {offset ^ last for offset in sent}, packet, other, last


def turn_kernel(tile, wq_hbm, wk_hbm, wv_hbm, *refs):
    out_ref, wq, wk, wv, sems = refs[-5:]
    steps = wq.shape[0] // tile
    copies = []
    for j in range(steps):
        rows = slice(j * tile, (j + 1) * tile)
        copies.append(
            [
                pltpu.make_async_copy(source.at[rows, :], target.at[rows, :], sems.at[j, i])
                for i, (source, target) in enumerate(
                    ((wq_hbm, wq), (wk_hbm, wk), (wv_hbm, wv))
                )
            ]
        )
        for copy in copies[j]:
            copy.start()
    for j in range(steps):
        rows = slice(j * tile, (j + 1) * tile)
        first = 0
        for copy, weight in zip(copies[j], (wq, wk, wv)):
            copy.wait()
            out_ref[first : first + weight.shape[1], rows] = weight[rows, :].T
            first += weight.shape[1]


def turn_weights(weights, after):
    features = weights[0].shape[0]
    widths = [w.shape[1] for w in weights]
    tile = min(512, features)
    hbm = pl.BlockSpec(memory_space=pltpu.HBM)
    return pl.pallas_call(
        functools.partial(turn_kernel, tile),
        out_shape=pltpu.VMEM((sum(widths), features), jnp.bfloat16),
        in_specs=[hbm] * 3 + [pl.BlockSpec(memory_space=pl.ANY)] * len(after),
        out_specs=pl.BlockSpec(memory_space=pltpu.VMEM),
        scratch_shapes=[pltpu.VMEM((features, width), jnp.bfloat16) for width in widths]
        + [pltpu.SemaphoreType.DMA((features // tile, 3))],
        compiler_params=pltpu.CompilerParams(vmem_limit_bytes=16 * MIB),
        cost_estimate=pl.CostEstimate(
            flops=0, bytes_accessed=4 * features * sum(widths), transcendentals=0
        ),
        name="turn_weights",
    )(*[pltpu.with_memory_space_constraint(w, pltpu.HBM) for w in weights], *after)


def early_kernel(columns, tile, *refs):
    count, width = len(columns[0]), refs[-1].shape[1] // 2
    w_ref, out_ref, gq = refs[2 * count :]
    tokens = refs[0].shape[0]
    for i in range(2):
        for k, first in enumerate(columns[i]):
            gq[k * tokens : (k + 1) * tokens, i * width : (i + 1) * width] = refs[
                i * count + k
            ][:, first : first + width]
    for j in range(w_ref.shape[1] // tile):
        cols = slice(j * tile, (j + 1) * tile)
        out_ref[:, cols] = contract(gq[...], w_ref[: 2 * width, cols], 1, 0).astype(
            jnp.bfloat16
        )


def early_product(pieces, blocks, width, weights):
    arrays = [side[b][0] for side in pieces for b in blocks]
    columns = [[side[b][1] for b in blocks] for side in pieces]
    tokens = arrays[0].shape[0]
    features = weights.shape[1]
    tile = min(1024, features)
    rows = len(blocks) * tokens
    vmem = pl.BlockSpec(memory_space=pltpu.VMEM)
    return pl.pallas_call(
        functools.partial(early_kernel, columns, tile),
        out_shape=jax.ShapeDtypeStruct((rows, features), jnp.bfloat16),
        in_specs=[vmem] * (len(arrays) + 1),
        out_specs=vmem,
        scratch_shapes=[pltpu.VMEM((rows, 2 * width), jnp.bfloat16)],
        compiler_params=pltpu.CompilerParams(vmem_limit_bytes=16 * MIB),
        cost_estimate=pl.CostEstimate(
            flops=4 * rows * features * width,
            bytes_accessed=4 * features * width + 2 * rows * features + 4 * rows * width,
            transcendentals=0,
        ),
        name="early_product",
    )(*arrays, weights)


def put_pair(target_ref, target, first, sums, offsets, blocks, b, start):
    count = target.stop - target.start
    if offsets is None:
        tokens = sums[0].shape[0] // blocks
        rows = pl.ds(pl.multiple_of(b * tokens + start, 16), count)
        target_ref[target, first:] = sums[0][rows, :]
        return
    rows = pl.ds(pl.multiple_of(start, 16), count)
    for i in range(2):
        cols = slice(first + i * HEAD_SIZE, first + (i + 1) * HEAD_SIZE)
        target_ref[target, cols] = summed_block(
            sums[2 * i], sums[2 * i + 1], blocks, b, offsets[i], rows
        )


def by_destination(blocks, half, place_ref, put):
    core, turn = place_ref[0], place_ref[1]
    for q in range(blocks):
        for b in range(blocks):

            @pl.when((q ^ turn) == b)
            def _():
                for side in range(2):
                    first = (side * blocks + q) * half
                    put(q, side, slice(first, first + half), b, (core ^ side) * half)


def place_in(members, b):
    place, found = jnp.int32(0), jnp.bool_(False)
    for i, member in enumerate(members):
        place = jnp.where(b == member, i, place)
        found = found | (b == member)
    return place, found


def last_kernel(early, late, columns, offsets, part, width, spare, place_ref, *refs):
    blocks = len(early) + len(late)
    early_ref, w_ref, refs = refs[0], refs[1], refs[2 + spare :]
    pieces = [refs[i * len(late) : (i + 1) * len(late)] for i in range(2)]
    refs = refs[2 * len(late) :]
    count = 1 if offsets is None else 4
    sums, refs = refs[:count], refs[count:]
    mine_refs, other_ref, gq, gkv, query, pair = refs[:blocks], *refs[blocks:]
    half = mine_refs[0].shape[0]
    tokens = 2 * half
    cols = slice(part * other_ref.shape[1], (part + 1) * other_ref.shape[1])

    for i in range(2):
        for k, first in enumerate(columns[i]):
            gq[k * tokens : (k + 1) * tokens, i * width : (i + 1) * width] = pieces[i][k][
                :, first : first + width
            ]

    core, turn = place_ref[0], place_ref[1]
    targets = [
        (q, side, slice((side * blocks + q) * half, (side * blocks + q + 1) * half))
        for q in range(blocks)
        for side in range(2)
    ]
    for q, side, target in targets:
        put_pair(gkv, target, 0, sums, offsets, blocks, q ^ turn, (core ^ side) * half)
    query[...] = contract(gq[...], w_ref[: 2 * width, cols], 1, 0).astype(jnp.bfloat16)
    pair[...] = contract(gkv[...], w_ref[2 * width :, cols], 1, 0)

    for q, side, target in targets:
        early_place, in_early = place_in(early, q ^ turn)
        late_place, in_late = place_in(late, q ^ turn)
        out_ref = other_ref.at[q * half : (q + 1) * half, :] if side else mine_refs[q]

        def put(part_ref, place, part_cols):
            start = place * tokens + (core ^ side) * half
            rows = pl.ds(pl.multiple_of(start, 16), half)
            total = pair[target, :] + part_ref[rows, part_cols].astype(jnp.float32)
            out_ref[...] = total.astype(jnp.bfloat16)

        pl.when(in_early)(functools.partial(put, early_ref, early_place, cols))
        pl.when(in_late)(functools.partial(put, query, late_place, slice(None)))


def last_product(place, early, late, early_part, pieces, sums, offsets, weights, width, part, after):
    blocks = len(early) + len(late)
    arrays = [side[b][0] for side in pieces for b in late]
    columns = [[side[b][1] for b in late] for side in pieces]
    tokens = arrays[0].shape[0]
    half, cols = tokens // 2, weights.shape[1] // 2
    pair_cols = weights.shape[0] - 2 * width
    vmem = pl.BlockSpec(memory_space=pltpu.VMEM)
    *mine, other = pl.pallas_call(
        functools.partial(
            last_kernel, early, late, columns, offsets, part, width, len(after)
        ),
        out_shape=[jax.ShapeDtypeStruct((half, cols), jnp.bfloat16)] * blocks
        + [jax.ShapeDtypeStruct((blocks * half, cols), jnp.bfloat16)],
        in_specs=[pl.BlockSpec(memory_space=pltpu.SMEM)]
        + [vmem] * 2
        + [pl.BlockSpec(memory_space=pl.ANY)] * len(after)
        + [vmem] * (len(arrays) + len(sums)),
        out_specs=[vmem] * (blocks + 1),
        scratch_shapes=[
            pltpu.VMEM((len(late) * tokens, 2 * width), jnp.bfloat16),
            pltpu.VMEM((blocks * tokens, pair_cols), jnp.bfloat16),
            pltpu.VMEM((len(late) * tokens, cols), jnp.bfloat16),
            pltpu.VMEM((blocks * tokens, cols), jnp.float32),
        ],
        compiler_params=pltpu.CompilerParams(vmem_limit_bytes=16 * MIB),
        cost_estimate=pl.CostEstimate(
            flops=2 * tokens * cols * (len(late) * 2 * width + blocks * pair_cols),
            bytes_accessed=2 * cols * (2 * width + pair_cols) + 8 * blocks * tokens * cols,
            transcendentals=0,
        ),
        name="last_product",
    )(place, early_part, weights, *after, *arrays, *sums)
    return mine, other


def order_kernel(blocks, columns, offsets, width, place_ref, *refs):
    pieces = [refs[i * blocks : (i + 1) * blocks] for i in range(2)]
    sums, g = refs[2 * blocks : -2], refs[-1]
    half = g.shape[0] // (2 * blocks)

    def put(q, side, target, b, start):
        rows = pl.ds(pl.multiple_of(start, 16), half)
        for i in range(2):
            first = columns[i][b]
            g[target, i * width : (i + 1) * width] = pieces[i][b][rows, first : first + width]
        put_pair(g, target, 2 * width, sums, offsets, blocks, b, start)

    by_destination(blocks, half, place_ref, put)


def order_rows(place, pieces, sums, offsets, width, cols, after):
    blocks = len(pieces[0])
    arrays = [side[b][0] for side in pieces for b in range(blocks)]
    columns = [[side[b][1] for b in range(blocks)] for side in pieces]
    rows = blocks * arrays[0].shape[0]
    vmem = pl.BlockSpec(memory_space=pltpu.VMEM)
    return pl.pallas_call(
        functools.partial(order_kernel, blocks, columns, offsets, width),
        out_shape=jax.ShapeDtypeStruct((rows, cols), jnp.bfloat16),
        in_specs=[pl.BlockSpec(memory_space=pltpu.SMEM)]
        + [vmem] * (len(arrays) + len(sums))
        + [pl.BlockSpec(memory_space=pl.ANY)],
        out_specs=vmem,
        compiler_params=pltpu.CompilerParams(vmem_limit_bytes=8 * MIB),
        cost_estimate=pl.CostEstimate(
            flops=0, bytes_accessed=4 * rows * cols, transcendentals=0
        ),
        name="order_rows",
    )(place, *arrays, *sums, after)


def join_kernel(count, *refs):
    sources, out_ref, sems = refs[:count], refs[count + 1], refs[count + 2]
    rows = sources[0].shape[0]
    copies = [
        pltpu.make_async_copy(source, out_ref.at[i * rows : (i + 1) * rows, :], sems.at[i])
        for i, source in enumerate(sources)
    ]
    for copy in copies:
        copy.start()
    for copy in copies:
        copy.wait()


def join_rows(arrays, after):
    count = len(arrays)
    rows, cols = arrays[0].shape
    return pl.pallas_call(
        functools.partial(join_kernel, count),
        out_shape=jax.ShapeDtypeStruct((count * rows, cols), arrays[0].dtype),
        in_specs=[pl.BlockSpec(memory_space=pl.ANY)] * (count + 1),
        out_specs=pl.BlockSpec(memory_space=pltpu.VMEM),
        scratch_shapes=[pltpu.SemaphoreType.DMA((count,))],
        compiler_params=pltpu.CompilerParams(vmem_limit_bytes=4 * MIB),
        cost_estimate=pl.CostEstimate(
            flops=0, bytes_accessed=4 * count * rows * cols, transcendentals=0
        ),
        name="join_rows",
    )(*arrays, after)


def weight_grad_kernel(places, g_ref, *refs):
    pieces = len(places)
    x_refs = refs[:pieces]
    gwq_ref, gwk_ref, gwv_ref, x_all = refs[pieces:]
    query_cols, key_cols = gwq_ref.shape[1], gwk_ref.shape[1]
    rows = x_refs[0].shape[0]
    for place, x_ref in zip(places, x_refs):
        x_all[place * rows : (place + 1) * rows, :] = x_ref[...]
    x = x_all[...]
    gwq_ref[...] = contract(x, g_ref[:, :query_cols], 0, 0)
    pair = contract(x, g_ref[:, query_cols:], 0, 0)
    gwk_ref[...] = pair[:, :key_cols]
    gwv_ref[...] = pair[:, key_cols:]


def weight_grads(g, x_parts, order, query_cols):
    chips = len(order)
    features = x_parts[0].shape[1]
    piece_tokens = g.shape[0] // (2 * chips)
    places = [core * chips + q for core in range(2) for q in order]
    counts = [part.shape[0] // piece_tokens for part in x_parts]
    key_cols = (g.shape[1] - query_cols) // 2
    tile = min(256, features)
    return pl.pallas_call(
        functools.partial(weight_grad_kernel, places),
        grid=(features // tile,),
        out_shape=[
            jax.ShapeDtypeStruct((features, query_cols), jnp.float32),
            jax.ShapeDtypeStruct((features, key_cols), jnp.float32),
            jax.ShapeDtypeStruct((features, key_cols), jnp.float32),
        ],
        in_specs=[pl.BlockSpec(g.shape, lambda i: (0, 0))]
        + [
            pl.BlockSpec((piece_tokens, tile), lambda i, k=k: (k, i))
            for count in counts
            for k in range(count)
        ],
        out_specs=[
            pl.BlockSpec((tile, query_cols), lambda i: (i, 0)),
            pl.BlockSpec((tile, key_cols), lambda i: (i, 0)),
            pl.BlockSpec((tile, key_cols), lambda i: (i, 0)),
        ],
        scratch_shapes=[pltpu.VMEM((g.shape[0], tile), jnp.bfloat16)],
        compiler_params=pltpu.CompilerParams(vmem_limit_bytes=32 * MIB),
        cost_estimate=pl.CostEstimate(
            flops=2 * g.size * features,
            bytes_accessed=2 * g.size + 2 * g.shape[0] * features + 4 * features * g.shape[1],
            transcendentals=0,
        ),
        name="weight_grads",
    )(g, *[x for x, n in zip(x_parts, counts) for _ in range(n)])


def sum_kernel(count, groups, *refs):
    out_ref = refs[-1]
    for i in range(groups):
        cols = slice(
            i * out_ref.shape[1] // groups, (i + 1) * out_ref.shape[1] // groups
        )
        total = refs[i * count][...].astype(jnp.float32)
        for ref in refs[i * count + 1 : (i + 1) * count]:
            total += ref[...].astype(jnp.float32)
        for ref in refs[groups * count : -2]:
            total += ref[:, cols].astype(jnp.float32)
        out_ref[:, cols] = total.astype(out_ref.dtype)


def sum_rows(groups, whole, after):
    rows, cols = groups[0][0].shape
    terms = [term for group in groups for term in group] + whole
    vmem = pl.BlockSpec(memory_space=pltpu.VMEM)
    return pl.pallas_call(
        functools.partial(sum_kernel, len(groups[0]), len(groups)),
        out_shape=jax.ShapeDtypeStruct((rows, cols * len(groups)), jnp.bfloat16),
        in_specs=[vmem] * len(terms) + [pl.BlockSpec(memory_space=pl.ANY)],
        out_specs=vmem,
        compiler_params=pltpu.CompilerParams(vmem_limit_bytes=4 * MIB),
        cost_estimate=pl.CostEstimate(
            flops=len(terms) * rows * cols,
            bytes_accessed=4 * len(terms) * rows * cols,
            transcendentals=0,
        ),
        name="sum_rows",
    )(*terms, pltpu.with_memory_space_constraint(after, pltpu.HBM))


def shards(
    layer_input,
    w_query,
    w_key,
    w_value,
    rotated_query_state,
    rotated_key_state,
    saved_value_state,
    context_gradient,
    positions,
    segment_ids,
):
    tokens = rotated_query_state.shape[0]
    n_row, n_col = lax.axis_size("row"), lax.axis_size("col")
    chips = n_col // 2
    shared_heads = n_col // KEY_VALUE_HEADS
    row_index = lax.axis_index("row").astype(jnp.int32)
    col_index = lax.axis_index("col").astype(jnp.int32)
    chip_index, core_index = col_index // 2, col_index % 2

    key, value = rotated_key_state, saved_value_state
    if shared_heads > 1:
        pair = jnp.concatenate([key, value], axis=1)
        pair = [pair] + [swap(pair, "col", s) for s in range(1, shared_heads)]
        part = col_index % shared_heads
        stacked = jnp.stack(pair)
        stacked = jnp.take(stacked, jnp.arange(shared_heads) ^ part, axis=0)
        stacked = stacked.reshape(shared_heads, tokens, 2, -1).transpose(1, 2, 0, 3)
        stacked = stacked.reshape(tokens, 2, HEAD_SIZE)
        key, value = stacked[:, 0], stacked[:, 1]
    packed = gather_direct(pack(key, value, segment_ids), "row")

    row = row_index.reshape(1)
    query, out_grad, cosine, sine = prepare(
        row, n_row, rotated_query_state, context_gradient, positions, segment_ids
    )
    first, second, *packets = attention_backward(row, query, out_grad, packed, cosine, sine)
    bits = [1 << i for i in range(n_row.bit_length() - 1)]
    pieces, sums, offsets, late = [], [], [], set()
    for own, packet, order in zip((first, second), packets, (bits, bits[::-1])):
        held, with_last, *last_two, offset = spread(own, packet, order, n_row)
        pieces.append(held)
        late |= with_last
        sums += last_two
        offsets.append(offset)

    if shared_heads > 1:
        dkv = []
        for i in range(2):
            packet, other = (a[:, -n_row * HEAD_SIZE :] for a in sums[2 * i : 2 * i + 2])
            packet, other = (a.reshape(tokens, n_row, HEAD_SIZE) for a in (packet, other))
            dkv.append(add_low(packet, other[:, np.arange(n_row) ^ offsets[i]]))
        dkv = jnp.stack(dkv, axis=2)
        bit = shared_heads // 2
        while bit:
            half = dkv.shape[3] // 2
            upper = (col_index & bit) != 0
            lower_part, upper_part = dkv[..., :half], dkv[..., half:]
            kept = jnp.where(upper, upper_part, lower_part)
            sent = jnp.where(upper, lower_part, upper_part)
            dkv = add_low(kept, swap(sent, "col", bit))
            bit //= 2
        sums, offsets = [dkv.transpose(1, 0, 2, 3).reshape(n_row * tokens, -1)], None

    held, order = layer_input, [0]
    bit = chips // 2
    while bit > 1:
        held = join_rows([held, swap(held, "col", 2 * bit)], first)
        order += [q | bit for q in order]
        bit //= 2
    x_parts = [held, swap(held, "col", 2)]
    order += [q | 1 for q in order]

    place = jnp.stack([core_index, row_index ^ chip_index])
    weights = turn_weights((w_query, w_key, w_value), [sums[0]])
    weights = pltpu.with_memory_space_constraint(weights, pltpu.VMEM)
    width = first.shape[1]
    early = [b for b in range(n_row) if b not in late]
    late = sorted(late)
    early_part = early_product(pieces, early, width, weights)
    half = tokens // 2
    groups, after = [], x_parts
    for part in range(2):
        mine, other = last_product(
            place, early, late, early_part, pieces, sums, offsets, weights, width, part, after
        )
        after = mine[:1]
        other = swap(other, "col", 1)
        group = {
            q: add_low(mine[q], other[q * half : (q + 1) * half]) for q in range(chips)
        }
        groups.append(group)
    x_parts += [swap(part, "col", 1) for part in x_parts]
    cols = weights.shape[0]
    g = order_rows(place, pieces, sums, offsets, width, cols, groups[1][chips - 1])
    terms = [[group.pop(0)] for group in groups]
    whole = []
    bit = 1
    while bit < chips:
        for q in sorted((q for q in groups[0] if q & bit), reverse=True):
            sent = [group.pop(q) for group in groups]
            if q == bit and 2 * bit < chips:
                sent = jnp.concatenate(sent, axis=1)
                sent = lax.optimization_barrier((sent, received))[0]
                whole.append(swap(sent, "col", 2 * bit))
                continue
            for group, term, half_sent in zip(groups, terms, sent):
                received = swap(half_sent, "col", 2 * bit)
                if q == bit:
                    term.append(received)
                else:
                    group[q ^ bit] = add_low(group[q ^ bit], received)
        bit *= 2

    grad_wq, grad_wk, grad_wv = weight_grads(g, x_parts, order, w_query.shape[1])
    grad_input = sum_rows(terms, whole, grad_wk)
    return grad_input, grad_wq, grad_wk, grad_wv


def solution(mesh):
    return jax.shard_map(
        shards,
        mesh=mesh,
        in_specs=(
            P("col", "row"),
            P("row", "col"),
            P("row", "col"),
            P("row", "col"),
            P("row", "col"),
            P("row", "col"),
            P("row", "col"),
            P("row", "col"),
            P("row"),
            P("row"),
        ),
        out_specs=(P("col", "row"), P("row", "col"), P("row", "col"), P("row", "col")),
        check_vma=False,
    )
```
